512 devices in a mesh: dp: 4 (over x), mx: 16 (over z_hi, y), my: 8 (over z_lo, core).
Axes of the slice: x: 4, y: 4, z: 16 (z_hi: 4, z_lo: 4; z = z_hi * 4 + z_lo), core: 2. Of those that a mesh axis runs over, the one named last changes fastest.
Arguments:
- normed: bfloat16 [2048, 6144], P(('dp', 'mx'), 'my'), may hold values from -6 to 6
- cotangent: bfloat16 [2048, 6144], P(('dp', 'mx'), 'my'), may hold values from -3 to 3
- w_in: bfloat16 [6144, 12288], P('my', 'mx'), may hold values from -0.078125 to 0.078125
- w_out: bfloat16 [12288, 6144], P('mx', 'my'), may hold values from -0.0546875 to 0.0546875
Outputs:
- normed_grad: bfloat16 [2048, 6144], P(('dp', 'mx'), 'my')
- w_in_grad: float32 [6144, 12288], P('my', ('mx', 'dp'))
- w_out_grad: float32 [12288, 6144], P(('mx', 'dp'), 'my')
The draws below stay inside these ranges and needn't reach their ends.
All inputs are finite; a program needn't handle non-finite values.
Results may differ from the reference program's by a relative error of at most 0.029.
Values may be sent and summed in bfloat16 or wider, within the bound.
A program may use at most 64 MiB of HBM per device.

```python
import jax
import jax.numpy as jnp
from jax import lax

D = 6144
F = 12288
TOK_DP = 512
TOKENS = 2048
N_DP = 4
N_MX = 16
N_MY = 8


def block_levels(rng, extent, split, smallest, largest):
    gain, own = 1.0, jax.random.fold_in(rng, 6)
    for dim, blocks in split:
        steps = jnp.exp(jax.random.uniform(jax.random.fold_in(own, dim), (blocks,), jnp.float32, smallest / len(split), largest / len(split)))
        gain = gain * jnp.repeat(steps, extent[dim] // blocks).reshape([-1 if axis == dim else 1 for axis in range(len(extent))])
    return gain


def noise(stream_key, extent, scale, limit, split=(), kind=jnp.bfloat16):
    result = jax.random.normal(stream_key, extent, jnp.float32) * scale
    if len(split) > 0:
        result = block_levels(stream_key, extent, split, -0.22, 0.18) * result
    return jnp.clip(result, min=-limit, max=limit).astype(kind)


def setup_inputs(seed: int = 0) -> dict:
    streams_of = jax.random.split(jax.random.key(seed), 5)
    return {
        "normed": noise(streams_of[0], (TOKENS, D), 1.0, 6.0, ((0, 64), (1, 8))),
        "cotangent": noise(streams_of[1], (TOKENS, D), 0.5, 3.0, ((0, 64), (1, 8))),
        "w_in": noise(streams_of[2], (D, F), D ** -0.5, 0.078125, ((0, 8), (1, 16))),
        "w_out": noise(streams_of[3], (F, D), F ** -0.5, 0.0546875, ((0, 16), (1, 8))),
    }


def rounded(value):
    return lax.optimization_barrier(value.astype(jnp.bfloat16)).astype(jnp.float32)


def block_sum(left_blocks, right_blocks, shape):
    def step(total, pair):
        return total + rounded(jnp.dot(pair[0], pair[1], preferred_element_type=jnp.float32)), None
    total, _ = lax.scan(step, jnp.zeros(shape, jnp.float32), (left_blocks, right_blocks))
    return total


def reference(normed, cotangent, w_in, w_out):
    width_my = D // N_MY
    width_mx = F // N_MX
    normed_blocks = normed.reshape(TOKENS, N_MY, width_my).transpose(1, 0, 2)
    cot_blocks = cotangent.reshape(TOKENS, N_MY, width_my).transpose(1, 0, 2)
    preact = block_sum(normed_blocks, w_in.reshape(N_MY, width_my, F), (TOKENS, F))
    out_blocks = w_out.reshape(F, N_MY, width_my).transpose(1, 2, 0)
    upstream = block_sum(cot_blocks, out_blocks, (TOKENS, F))
    cumulative = 0.5 * (1.0 + lax.erf(preact * 0.7071067811865476))
    density = jnp.exp(-0.5 * preact * preact) * 0.3989422804014327
    activation = (preact * cumulative).astype(jnp.bfloat16)
    hidden_grad = (upstream * (cumulative + preact * density)).astype(jnp.bfloat16)
    grad_blocks = hidden_grad.reshape(TOKENS, N_MX, width_mx).transpose(1, 0, 2)
    in_blocks = w_in.reshape(D, N_MX, width_mx).transpose(1, 2, 0)
    normed_grad = block_sum(grad_blocks, in_blocks, (TOKENS, D)).astype(jnp.bfloat16)
    normed_shards = normed.reshape(N_DP, TOK_DP, D).transpose(0, 2, 1)
    w_in_grad = block_sum(normed_shards, hidden_grad.reshape(N_DP, TOK_DP, F), (D, F))
    act_shards = activation.reshape(N_DP, TOK_DP, F).transpose(0, 2, 1)
    w_out_grad = block_sum(act_shards, cotangent.reshape(N_DP, TOK_DP, D), (F, D))
    return normed_grad, w_in_grad, w_out_grad
```

```python
import jax
import jax.numpy as jnp
from jax import lax
from jax.experimental import pallas as pl
from jax.experimental.pallas import tpu as pltpu
from jax.sharding import PartitionSpec as P

MESH = pl.DeviceIdType.MESH
BF16, F32 = jnp.bfloat16, jnp.float32

NC = 6
TOK = 512
ROWS = 32
DM = 768
FH = 768
FC = FH // NC
Q = FC // 4
HALF = DM // 2

S_BWD = 8
S_X2 = 9
S_X3 = 10


def nt(a, b):
    return lax.dot_general(a, b, (((1,), (1,)), ((), ())), preferred_element_type=F32)


def nn(a, b):
    return lax.dot_general(a, b, (((1,), (0,)), ((), ())), preferred_element_type=F32)


def tn(a, b):
    return lax.dot_general(a, b, (((0,), (0,)), ((), ())), preferred_element_type=F32)


def activate(preact, upstream):
    cumulative = 0.5 * (1.0 + lax.erf(preact * 0.7071067811865476))
    density = jnp.exp(-0.5 * preact * preact) * 0.3989422804014327
    activation = (preact * cumulative).astype(BF16)
    hidden_grad = (upstream * (cumulative + preact * density)).astype(BF16)
    return activation, hidden_grad


def kernel(
    normed, cotangent, w_in, w_out,
    ng_out, win_out, wout_out,
    xg, win_v, w1t, wo, pu, crecv, zrecv, ah, dw, xr1, xr2, ng, ngb, yr1, yr2, zs, gz1, gz2,
    lsem, az_s, az_r, azf_s, azf_r, ay_s, ay_r, ayf_s, ayf_r,
    co_s, co_r, ch_s, ch_r, bc_s, bc_r, ce_s, ce_r, x1_s, x1_r, x2_s, x2_r,
    gy1_s, gy1_r, gy2_s, gy2_r, gz1_s, gz1_r, gz2_s, gz2_r,
):
    x = lax.axis_index("dp")
    mx = lax.axis_index("mx")
    my = lax.axis_index("my")
    zh, y = mx // 4, mx % 4
    zl, c = my // 2, my % 2
    o = 1 - c

    def at_x(k):
        return {"dp": (x + k) % 4}

    def at_y(k):
        return {"mx": zh * 4 + (y + k) % 4}

    def at_zh(k):
        return {"mx": ((zh + k) % 4) * 4 + y}

    def at_zl(k):
        return {"my": ((zl + k) % 4) * 2 + c}

    at_core = {"my": zl * 2 + o}

    def rc(src, dst, send, recv, device):
        return pltpu.make_async_remote_copy(
            src_ref=src, dst_ref=dst, send_sem=send, recv_sem=recv, device_id=device, device_id_type=MESH
        )

    load_in = pltpu.make_async_copy(w_in, win_v, lsem.at[4])
    load_in.start()
    load_out = [pltpu.make_async_copy(w_out.at[g], wo.at[:, g], lsem.at[g]) for g in range(4)]
    for copy in load_out:
        copy.start()

    barrier = pltpu.get_barrier_semaphore()
    partners = [at_core]
    for k in (1, 3):
        partners += [at_x(k), at_y(k), at_zh(k), at_zl(k)]
    for device in partners:
        pl.semaphore_signal(barrier, inc=1, device_id=device, device_id_type=MESH)
    pl.semaphore_wait(barrier, len(partners))

    STEP = (1, 3)

    def block(k, yy):
        return pl.ds(pl.multiple_of((((zh + k) % 4) * 4 + yy) * ROWS, ROWS), ROWS)

    def own(a):
        return (normed, cotangent)[a]

    def az(d, a):
        return rc(own(a), xg.at[a, block(0, y)], az_s.at[d, a], az_r.at[d, a], at_zh(STEP[d]))

    def az_wait(d, a):
        here = xg.at[a, block(STEP[1 - d], y)]
        rc(here, here, az_s.at[d, a], az_r.at[d, a], at_zh(STEP[d])).wait_recv()

    def azf(d):
        here = xg.at[d, block(STEP[1 - d], y)]
        return rc(here, here, azf_s.at[d], azf_r.at[d], at_zh(STEP[d]))

    def azf_wait(d):
        here = xg.at[d, block(2, y)]
        rc(here, here, azf_s.at[d], azf_r.at[d], at_zh(STEP[d])).wait_recv()

    def ay(k, d, a):
        src = own(a) if k == 0 else xg.at[a, block(k, y)]
        return rc(src, xg.at[a, block(k, y)], ay_s.at[k, d, a], ay_r.at[k, d, a], at_y(STEP[d]))

    def ay_wait(k, d, a):
        here = xg.at[a, block(k, (y + STEP[1 - d]) % 4)]
        rc(here, here, ay_s.at[k, d, a], ay_r.at[k, d, a], at_y(STEP[d])).wait_recv()

    def ayf(k, d):
        here = xg.at[d, block(k, (y + STEP[1 - d]) % 4)]
        return rc(here, here, ayf_s.at[k, d], ayf_r.at[k, d], at_y(STEP[d]))

    def ayf_wait(k, d):
        here = xg.at[d, block(k, (y + 2) % 4)]
        rc(here, here, ayf_s.at[k, d], ayf_r.at[k, d], at_y(STEP[d])).wait_recv()

    for a in range(2):
        az(0, a).start()
        az(1, 1 - a).start()
        ay(0, 0, a).start()
        ay(0, 1, 1 - a).start()
    for a in range(2):
        xg[a, block(0, y)] = own(a)[...]

    load_in.wait()
    for k in range(FH // 128):
        turned = win_v[:, k * 128:(k + 1) * 128].T
        for part in range(128 // Q):
            g, rest = divmod(k * 128 + part * Q, FH // 4)
            w1t[rest // Q, g] = turned[part * Q:(part + 1) * Q]
    for copy in load_out:
        copy.wait()

    for d in range(2):
        ay_wait(0, d, d)
        ayf(0, d).start()
    for d in range(2):
        az_wait(d, d)
        azf(d).start()
        for e in range(2):
            ay(STEP[1 - d], e, d).start()
    for d in range(2):
        az_wait(d, 1 - d)
        for e in range(2):
            ay(STEP[1 - d], e, 1 - d).start()
    for k in (3, 1):
        for d in range(2):
            ay_wait(k, d, d)
            ayf(k, d).start()
    for d in range(2):
        azf_wait(d)
        for e in range(2):
            ay(2, e, d).start()
    for d in range(2):
        ay_wait(2, d, d)
        ayf(2, d).start()
    for k in (0, 3, 1, 2):
        for d in range(2):
            ay_wait(k, d, 1 - d)
            ayf_wait(k, d)

    OWNER = (0, 3)
    TO_OWNER = (3, 1)
    ng[...] = jnp.zeros_like(ng)

    def core_copy(j):
        return rc(pu.at[j, o], crecv.at[j], co_s.at[j], co_r.at[j], at_core)

    def chain(j, side):
        return rc(pu.at[j, c, side], zrecv.at[j, side], ch_s.at[j, side], ch_r.at[j, side], at_zl(TO_OWNER[side]))

    def spread(j, side):
        here = ah.at[j, :, 2 * c + side]
        return rc(here, here, bc_s.at[j, side], bc_r.at[j, side], at_zl(TO_OWNER[1 - side]))

    def core_share(j, side):
        here = ah.at[j, :, 2 * c + side]
        return rc(here, here, ce_s.at[j, side], ce_r.at[j, side], at_core)

    def core_share_wait(j, side):
        here = ah.at[j, :, 2 * o + side]
        rc(here, here, ce_s.at[j, side], ce_r.at[j, side], at_core).wait_recv()

    def x1(j, d):
        return rc(dw.at[j, d, (x + 2) % 4], xr1.at[j, d], x1_s.at[j, d], x1_r.at[j, d], at_x(STEP[d]))

    def x2(j, d):
        return rc(dw.at[j, :, (x + STEP[d]) % 4], xr2.at[j, d], x2_s.at[j, d], x2_r.at[j, d], at_x(STEP[d]))

    def forward(j):
        for a, w in enumerate((w1t, wo)):
            part = nt(w[j].reshape(FC, DM), xg[a]).astype(BF16)
            for q in range(4):
                pu[j, q // 2, q % 2, a] = part[q * Q:(q + 1) * Q]
        core_copy(j).start()

    def add_core(j):
        core_copy(j).wait_recv()
        pu[j, c] = (pu[j, c].astype(F32) + crecv[j].astype(F32)).astype(BF16)
        for side in range(2):
            @pl.when(zl == OWNER[1 - side])
            def _():
                chain(j, side).start()

    def pass_on(j, side):
        chain(j, side).wait_recv()
        pu[j, c, side] = (pu[j, c, side].astype(F32) + zrecv[j, side].astype(F32)).astype(BF16)
        chain(j, side).start()

    def finish(j, side):
        chain(j, side).wait_recv()
        total = [pu[j, c, side, a].astype(F32) + zrecv[j, side, a].astype(F32) for a in range(2)]
        activation, hidden_grad = activate(*total)
        ah[j, 0, 2 * c + side] = activation
        ah[j, 1, 2 * c + side] = hidden_grad
        spread(j, side).start()
        core_share(j, side).start()

    def pass_back(j, side, last):
        spread(j, side).wait_recv()
        if not last:
            spread(j, side).start()
        core_share(j, side).start()

    def backward(j):
        for side in range(2):
            core_share_wait(j, side)
        hidden_grad = ah[j, 1].reshape(FC, TOK)
        dw[j, 0] = nn(hidden_grad, xg[0]).astype(BF16).reshape(4, Q, DM)
        x1(j, 0).start()
        dw[j, 1] = nn(ah[j, 0].reshape(FC, TOK), xg[1]).astype(BF16).reshape(4, Q, DM)
        x1(j, 1).start()
        ng[...] += tn(hidden_grad, w1t[j].reshape(FC, DM))

    def x_step2(j):
        for d in range(2):
            x1(j, d).wait_recv()
            to = (x + STEP[d]) % 4
            dw[j, d, to] = (dw[j, d, to].astype(F32) + xr1[j, d].astype(F32)).astype(BF16)
            x2(j, d).start()

    def x_step3(j):
        for d in range(2):
            x2(j, d).wait_recv()
        rows = pl.ds(pl.multiple_of(j * Q, Q), Q)
        for a, out in enumerate((win_out, wout_out)):
            out[rows] = dw[j, a, x].astype(F32) + xr2[j, 0, a].astype(F32) + xr2[j, 1, a].astype(F32)

    def step(tau, carry):
        def stage(s, run, on=None):
            j = tau - s
            here = (j >= 0) & (j < NC)
            if on is not None:
                here = here & (zl == on)

            @pl.when(here)
            def _():
                run(j)

        for side in range(2):
            at = (lambda i: i) if side == 0 else (lambda i: 3 - i)
            stage(7, lambda j: pass_back(j, side, True), at(3))
            stage(6, lambda j: pass_back(j, side, False), at(2))
            stage(5, lambda j: pass_back(j, side, False), at(1))
            stage(4, lambda j: finish(j, side), at(0))
            stage(3, lambda j: pass_on(j, side), at(1))
            stage(2, lambda j: pass_on(j, side), at(2))
        stage(1, add_core)
        stage(0, forward)
        stage(S_BWD, backward)
        stage(S_X2, x_step2)
        stage(S_X3, x_step3)
        return carry

    lax.fori_loop(0, NC + S_BWD, step, 0)

    for h in range(2):
        ngb[:, :, h] = ng[:, h * HALF:(h + 1) * HALF].astype(BF16).reshape(4, 4, ROWS, HALF)

    def y1(k, d):
        return rc(ngb.at[(zh + k) % 4, (y + 2) % 4, d], yr1.at[k, d], gy1_s.at[k, d], gy1_r.at[k, d], at_y(STEP[d]))

    def y2(k, d):
        to = ngb.at[(zh + k) % 4, (y + STEP[d]) % 4]
        return rc(to, yr2.at[k, d], gy2_s.at[k, d], gy2_r.at[k, d], at_y(STEP[d]))

    def z1(d):
        return rc(zs.at[2, d], gz1.at[d], gz1_s.at[d], gz1_r.at[d], at_zh(STEP[d]))

    def z2(d):
        return rc(zs.at[STEP[d]], gz2.at[d], gz2_s.at[d], gz2_r.at[d], at_zh(STEP[d]))

    order = (2, 1, 3, 0)
    for k in order:
        for d in range(2):
            y1(k, d).start()
    x_step2(NC - 1)
    for k in order:
        for d in range(2):
            y1(k, d).wait_recv()
            zz, to = (zh + k) % 4, (y + STEP[d]) % 4
            ngb[zz, to, d] = (ngb[zz, to, d].astype(F32) + yr1[k, d].astype(F32)).astype(BF16)
            y2(k, d).start()
    x_step3(NC - 2)
    for k in order:
        for d in range(2):
            y2(k, d).wait_recv()
        total = ngb[(zh + k) % 4, y].astype(F32) + yr2[k, 0].astype(F32) + yr2[k, 1].astype(F32)
        zs[k] = total.astype(BF16)
        if k == 2:
            for d in range(2):
                z1(d).start()
    for d in range(2):
        z1(d).wait_recv()
        k = STEP[d]
        zs[k, d] = (zs[k, d].astype(F32) + gz1[d].astype(F32)).astype(BF16)
        z2(d).start()
    x_step3(NC - 1)
    for d in range(2):
        z2(d).wait_recv()
    total = zs[0].astype(F32) + gz2[0].astype(F32) + gz2[1].astype(F32)
    for h in range(2):
        ng_out[:, h * HALF:(h + 1) * HALF] = total[h].astype(BF16)

    for d in range(2):
        for a in range(2):
            az(d, a).wait_send()
        azf(d).wait_send()
        for k in range(4):
            for a in range(2):
                ay(k, d, a).wait_send()
            ayf(k, d).wait_send()
            y1(k, d).wait_send()
            y2(k, d).wait_send()
        z1(d).wait_send()
        z2(d).wait_send()

    def sent(j, carry):
        core_copy(j).wait_send()
        for side in range(2):
            @pl.when(zl != OWNER[side])
            def _():
                chain(j, side).wait_send()

            @pl.when(zl != OWNER[1 - side])
            def _():
                spread(j, side).wait_send()

            core_share(j, side).wait_send()
            x1(j, side).wait_send()
            x2(j, side).wait_send()
        return carry

    lax.fori_loop(0, NC, sent, 0)


def per_device(normed, cotangent, w_in, w_out):
    vmem = pl.BlockSpec(memory_space=pltpu.VMEM)
    anywhere = pl.BlockSpec(memory_space=pl.ANY)
    two = lambda *shape: [pltpu.SemaphoreType.DMA(shape)] * 2
    ng, win_t, wout = pl.pallas_call(
        kernel,
        out_shape=(
            jax.ShapeDtypeStruct((ROWS, DM), BF16),
            jax.ShapeDtypeStruct((FH // 4, DM), F32),
            jax.ShapeDtypeStruct((FH // 4, DM), F32),
        ),
        in_specs=[vmem, vmem, anywhere, anywhere],
        out_specs=[vmem, vmem, vmem],
        scratch_shapes=[
            pltpu.VMEM((2, TOK, DM), BF16),
            pltpu.VMEM((DM, FH), BF16),
            pltpu.VMEM((NC, 4, Q, DM), BF16),
            pltpu.VMEM((NC, 4, Q, DM), BF16),
            pltpu.VMEM((NC, 2, 2, 2, Q, TOK), BF16),
            pltpu.VMEM((NC, 2, 2, Q, TOK), BF16),
            pltpu.VMEM((NC, 2, 2, Q, TOK), BF16),
            pltpu.VMEM((NC, 2, 4, Q, TOK), BF16),
            pltpu.VMEM((NC, 2, 4, Q, DM), BF16),
            pltpu.VMEM((NC, 2, Q, DM), BF16),
            pltpu.VMEM((NC, 2, 2, Q, DM), BF16),
            pltpu.VMEM((TOK, DM), F32),
            pltpu.VMEM((4, 4, 2, ROWS, HALF), BF16),
            pltpu.VMEM((4, 2, ROWS, HALF), BF16),
            pltpu.VMEM((4, 2, 2, ROWS, HALF), BF16),
            pltpu.VMEM((4, 2, ROWS, HALF), BF16),
            pltpu.VMEM((2, ROWS, HALF), BF16),
            pltpu.VMEM((2, 2, ROWS, HALF), BF16),
            pltpu.SemaphoreType.DMA((5,)),
            *two(2, 2), *two(2), *two(4, 2, 2), *two(4, 2),
            *two(NC), *two(NC, 2), *two(NC, 2), *two(NC, 2), *two(NC, 2), *two(NC, 2),
            *two(4, 2), *two(4, 2), *two(2), *two(2),
        ],
        compiler_params=pltpu.CompilerParams(
            collective_id=0, has_side_effects=True, vmem_limit_bytes=48 * 1024 * 1024
        ),
        name="mlp_branch",
    )(normed, cotangent, w_in, w_out.reshape(4, NC, Q, DM))
    return ng, win_t.T, wout


def solution(mesh):
    return jax.shard_map(
        per_device,
        mesh=mesh,
        in_specs=(P(("dp", "mx"), "my"), P(("dp", "mx"), "my"), P("my", "mx"), P("mx", "my")),
        out_specs=(P(("dp", "mx"), "my"), P("my", ("mx", "dp")), P(("mx", "dp"), "my")),
        check_vma=False,
    )
```

```python
import jax
import jax.numpy as jnp
from jax import lax
from jax.experimental import pallas as pl
from jax.experimental.pallas import tpu as pltpu
from jax.sharding import PartitionSpec as P

MESH = pl.DeviceIdType.MESH
BF16, F32 = jnp.bfloat16, jnp.float32

NC = 6
TOK = 512
ROWS = 32
PIECE = ROWS // 2
DM = 768
FH = 768
FC = FH // NC
Q = FC // 4
HALF = DM // 2

S_BWD = 5
S_X2 = 6
S_X3 = 7


def nt(a, b):
    return lax.dot_general(a, b, (((1,), (1,)), ((), ())), preferred_element_type=F32)


def nn(a, b):
    return lax.dot_general(a, b, (((1,), (0,)), ((), ())), preferred_element_type=F32)


def tn(a, b):
    return lax.dot_general(a, b, (((0,), (0,)), ((), ())), preferred_element_type=F32)


def activate(preact, upstream):
    cumulative = 0.5 * (1.0 + lax.erf(preact * 0.7071067811865476))
    density = jnp.exp(-0.5 * preact * preact) * 0.3989422804014327
    activation = (preact * cumulative).astype(BF16)
    hidden_grad = (upstream * (cumulative + preact * density)).astype(BF16)
    return activation, hidden_grad


def kernel(
    normed, cotangent, w_in, w_out,
    ng_out, win_out, wout_out,
    xg, win_v, w1t, wo, pu, crecv, zrecv, ah, dw, xr1, xr2, ng, ngb, yr1, yr2, zs, gz1, gz2,
    lsem, az_s, az_r, azf_s, azf_r, ay_s, ay_r, ayf_s, ayf_r,
    co_s, co_r, ne_s, ne_r, ch_s, ch_r, sn_s, sn_r, sp_s, sp_r, ce_s, ce_r, x1_s, x1_r, x2_s, x2_r,
    gy1_s, gy1_r, gy2_s, gy2_r, gz1_s, gz1_r, gz2_s, gz2_r,
):
    x = lax.axis_index("dp")
    mx = lax.axis_index("mx")
    my = lax.axis_index("my")
    zh, y = mx // 4, mx % 4
    zl, c = my // 2, my % 2
    o = 1 - c

    def at_x(k):
        return {"dp": (x + k) % 4}

    def at_y(k):
        return {"mx": zh * 4 + (y + k) % 4}

    def at_zh(k):
        return {"mx": ((zh + k) % 4) * 4 + y}

    def at_zl(k):
        return {"my": ((zl + k) % 4) * 2 + c}

    at_core = {"my": zl * 2 + o}

    def rc(src, dst, send, recv, device):
        return pltpu.make_async_remote_copy(
            src_ref=src, dst_ref=dst, send_sem=send, recv_sem=recv, device_id=device, device_id_type=MESH
        )

    STEP = (1, 3)

    def block(k, yy):
        return pl.ds(pl.multiple_of((((zh + k) % 4) * 4 + yy) * ROWS, ROWS), ROWS)

    def part(k, yy, r):
        return pl.ds(pl.multiple_of((((zh + k) % 4) * 4 + yy) * ROWS + r * PIECE, PIECE), PIECE)

    load_own = [pltpu.make_async_copy(t, xg.at[a, block(0, y)], lsem.at[5 + a]) for a, t in enumerate((normed, cotangent))]
    load_in = pltpu.make_async_copy(w_in, win_v, lsem.at[4])
    load_out = [pltpu.make_async_copy(w_out.at[g], wo.at[:, g], lsem.at[g]) for g in range(4)]
    for copy in (*load_own, load_in, *load_out):
        copy.start()

    barrier = pltpu.get_barrier_semaphore()
    partners = [at_core]
    for k in (1, 3):
        partners += [at_x(k), at_y(k), at_zh(k), at_zl(k)]
    for device in partners:
        pl.semaphore_signal(barrier, inc=1, device_id=device, device_id_type=MESH)
    pl.semaphore_wait(barrier, len(partners))

    def az(d, a, r):
        here = xg.at[a, part(0, y, r)]
        return rc(here, here, az_s.at[d, a, r], az_r.at[d, a, r], at_zh(STEP[d]))

    def az_wait(d, a, r):
        here = xg.at[a, part(STEP[1 - d], y, r)]
        rc(here, here, az_s.at[d, a, r], az_r.at[d, a, r], at_zh(STEP[d])).wait_recv()

    def azf(d, r):
        here = xg.at[d, part(STEP[1 - d], y, r)]
        return rc(here, here, azf_s.at[d, r], azf_r.at[d, r], at_zh(STEP[d]))

    def azf_wait(d, r):
        here = xg.at[d, part(2, y, r)]
        rc(here, here, azf_s.at[d, r], azf_r.at[d, r], at_zh(STEP[d])).wait_recv()

    def ay(k, d, a, r):
        here = xg.at[a, part(k, y, r)]
        return rc(here, here, ay_s.at[k, d, a, r], ay_r.at[k, d, a, r], at_y(STEP[d]))

    def ay_wait(k, d, a, r):
        here = xg.at[a, part(k, (y + STEP[1 - d]) % 4, r)]
        rc(here, here, ay_s.at[k, d, a, r], ay_r.at[k, d, a, r], at_y(STEP[d])).wait_recv()

    def ayf(k, d, r):
        here = xg.at[d, part(k, (y + STEP[1 - d]) % 4, r)]
        return rc(here, here, ayf_s.at[k, d, r], ayf_r.at[k, d, r], at_y(STEP[d]))

    def ayf_wait(k, d, r):
        here = xg.at[d, part(k, (y + 2) % 4, r)]
        rc(here, here, ayf_s.at[k, d, r], ayf_r.at[k, d, r], at_y(STEP[d])).wait_recv()

    for copy in load_own:
        copy.wait()
    for a in range(2):
        for r in range(2):
            az(0, a, r).start()
            az(1, 1 - a, r).start()
            ay(0, 0, a, r).start()
            ay(0, 1, 1 - a, r).start()

    load_in.wait()
    for k in range(FH // 128):
        turned = win_v[:, k * 128:(k + 1) * 128].T
        for u in range(128 // Q):
            g, rest = divmod(k * 128 + u * Q, FH // 4)
            w1t[rest // Q, g] = turned[u * Q:(u + 1) * Q]
    for copy in load_out:
        copy.wait()

    def along_y(k, a, r):
        for d in range(2):
            ay(k, d, a, r).start()

    def further_y(k, a, r):
        ay_wait(k, a, a, r)
        ayf(k, a, r).start()

    for r in range(2):
        for a in range(2):
            further_y(0, a, r)
    arrived = [[(0, 0, r), (1, 1, r)] for r in range(2)] + [[(0, 1, r), (1, 0, r)] for r in range(2)]
    previous = None
    for n, pieces in enumerate(arrived):
        for d, a, r in pieces:
            az_wait(d, a, r)
            if d == a:
                azf(d, r).start()
            along_y(STEP[1 - d], a, r)
        if previous is not None:
            for d, a, r in previous:
                further_y(STEP[1 - d], a, r)
        previous = pieces
    for r in range(2):
        for d in range(2):
            azf_wait(d, r)
            along_y(2, d, r)
        for d, a, rr in previous:
            further_y(2 if r else STEP[1 - d], a, rr)
        previous = [(d, d, r) for d in range(2)]
    for d, a, r in previous:
        further_y(2, a, r)
    for k in (0, 3, 1, 2):
        for d in range(2):
            for r in range(2):
                ay_wait(k, d, 1 - d, r)
                ayf_wait(k, d, r)

    NEAR, OWNER, RELAY, FAR = range(4)
    ng[...] = jnp.zeros_like(ng)

    def core_copy(j):
        return rc(pu.at[j, o], crecv.at[j], co_s.at[j], co_r.at[j], at_core)

    def near(j, side, a):
        return rc(
            pu.at[j, c, side, a], zrecv.at[j, side, 0, a], ne_s.at[j, side, a], ne_r.at[j, side, a], at_zl(STEP[side])
        )

    def chain(j, side, a):
        return rc(
            pu.at[j, c, side, a], zrecv.at[j, side, 1, a], ch_s.at[j, side, a], ch_r.at[j, side, a], at_zl(STEP[1 - side])
        )

    def spread_near(j, side, a):
        here = ah.at[j, a, 2 * c + side]
        return rc(here, here, sn_s.at[j, side, a], sn_r.at[j, side, a], at_zl(STEP[1 - side]))

    def spread(j, side, a):
        here = ah.at[j, a, 2 * c + side]
        return rc(here, here, sp_s.at[j, side, a], sp_r.at[j, side, a], at_zl(STEP[side]))

    def core_share(j, side):
        here = ah.at[j, :, 2 * c + side]
        return rc(here, here, ce_s.at[j, side], ce_r.at[j, side], at_core)

    def core_share_wait(j, side):
        here = ah.at[j, :, 2 * o + side]
        rc(here, here, ce_s.at[j, side], ce_r.at[j, side], at_core).wait_recv()

    def x1(j, d):
        return rc(dw.at[j, d, (x + 2) % 4], xr1.at[j, d], x1_s.at[j, d], x1_r.at[j, d], at_x(STEP[d]))

    def x2(j, d):
        return rc(dw.at[j, :, (x + STEP[d]) % 4], xr2.at[j, d], x2_s.at[j, d], x2_r.at[j, d], at_x(STEP[d]))

    def forward(j):
        for a, w in enumerate((w1t, wo)):
            part = nt(w[j].reshape(FC, DM), xg[a]).astype(BF16)
            for q in range(4):
                pu[j, q // 2, q % 2, a] = part[q * Q:(q + 1) * Q]
        core_copy(j).start()

    def place(side):
        return zl if side == 0 else 3 - zl

    def add_core(j):
        core_copy(j).wait_recv()
        pu[j, c] = (pu[j, c].astype(F32) + crecv[j].astype(F32)).astype(BF16)
        for side in range(2):
            @pl.when(place(side) == FAR)
            def _():
                for a in range(2):
                    chain(j, side, a).start()
                for a in range(2):
                    near(j, 1 - side, a).start()

    def pass_on(j, side):
        for a in range(2):
            chain(j, side, a).wait_recv()
            pu[j, c, side, a] = (pu[j, c, side, a].astype(F32) + zrecv[j, side, 1, a].astype(F32)).astype(BF16)
            chain(j, side, a).start()

    def finish(j, side):
        total = []
        for a in range(2):
            chain(j, side, a).wait_recv()
            near(j, side, a).wait_recv()
            total.append(
                pu[j, c, side, a].astype(F32) + zrecv[j, side, 0, a].astype(F32) + zrecv[j, side, 1, a].astype(F32)
            )
        for a, value in enumerate(activate(*total)):
            ah[j, a, 2 * c + side] = value
        for a in range(2):
            spread(j, side, a).start()
        for a in range(2):
            spread_near(j, side, a).start()
        core_share(j, side).start()

    def pass_back(j, side):
        for a in range(2):
            spread(j, side, a).wait_recv()
            spread(j, side, a).start()
        core_share(j, side).start()

    def take_far(j, side):
        for a in range(2):
            spread(j, side, a).wait_recv()
        core_share(j, side).start()

    def take_near(j, side):
        for a in range(2):
            spread_near(j, side, a).wait_recv()
        core_share(j, side).start()

    def backward(j):
        for side in range(2):
            core_share_wait(j, side)
        hidden_grad = ah[j, 1].reshape(FC, TOK)
        dw[j, 0] = nn(hidden_grad, xg[0]).astype(BF16).reshape(4, Q, DM)
        x1(j, 0).start()
        dw[j, 1] = nn(ah[j, 0].reshape(FC, TOK), xg[1]).astype(BF16).reshape(4, Q, DM)
        x1(j, 1).start()
        ng[...] += tn(hidden_grad, w1t[j].reshape(FC, DM))

    def x_step2(j):
        for d in range(2):
            x1(j, d).wait_recv()
            to = (x + STEP[d]) % 4
            dw[j, d, to] = (dw[j, d, to].astype(F32) + xr1[j, d].astype(F32)).astype(BF16)
            x2(j, d).start()

    def x_step3(j):
        for d in range(2):
            x2(j, d).wait_recv()
        rows = pl.ds(pl.multiple_of(j * Q, Q), Q)
        for a, out in enumerate((win_out, wout_out)):
            out[rows] = dw[j, a, x].astype(F32) + xr2[j, 0, a].astype(F32) + xr2[j, 1, a].astype(F32)

    def step(tau, carry):
        def stage(s, run, on=None):
            j = tau - s
            here = (j >= 0) & (j < NC)
            if on is not None:
                here = here & (place(on[0]) == on[1])

            @pl.when(here)
            def _():
                run(j)

        for side in range(2):
            stage(5, lambda j: take_far(j, side), (side, FAR))
            stage(4, lambda j: pass_back(j, side), (side, RELAY))
            stage(4, lambda j: take_near(j, side), (side, NEAR))
        for side in range(2):
            stage(3, lambda j: finish(j, side), (side, OWNER))
        for side in range(2):
            stage(2, lambda j: pass_on(j, side), (side, RELAY))
        stage(1, add_core)
        stage(0, forward)
        stage(S_BWD, backward)
        stage(S_X2, x_step2)
        stage(S_X3, x_step3)
        return carry

    lax.fori_loop(0, NC + S_BWD, step, 0)

    for h in range(2):
        ngb[:, :, h] = ng[:, h * HALF:(h + 1) * HALF].astype(BF16).reshape(4, 4, ROWS, HALF)

    def y1(k, d):
        return rc(ngb.at[(zh + k) % 4, (y + 2) % 4, d], yr1.at[k, d], gy1_s.at[k, d], gy1_r.at[k, d], at_y(STEP[d]))

    def y2(k, d):
        to = ngb.at[(zh + k) % 4, (y + STEP[d]) % 4]
        return rc(to, yr2.at[k, d], gy2_s.at[k, d], gy2_r.at[k, d], at_y(STEP[d]))

    def z1(d):
        return rc(zs.at[2, d], gz1.at[d], gz1_s.at[d], gz1_r.at[d], at_zh(STEP[d]))

    def z2(d):
        return rc(zs.at[STEP[d]], gz2.at[d], gz2_s.at[d], gz2_r.at[d], at_zh(STEP[d]))

    def along_y1(k):
        for d in range(2):
            y1(k, d).start()

    def along_y2(k):
        for d in range(2):
            y1(k, d).wait_recv()
            zz, to = (zh + k) % 4, (y + STEP[d]) % 4
            ngb[zz, to, d] = (ngb[zz, to, d].astype(F32) + yr1[k, d].astype(F32)).astype(BF16)
            y2(k, d).start()

    def sum_y(k):
        for d in range(2):
            y2(k, d).wait_recv()
        total = ngb[(zh + k) % 4, y].astype(F32) + yr2[k, 0].astype(F32) + yr2[k, 1].astype(F32)
        zs[k] = total.astype(BF16)

    for k in (2, 1, 3, 0):
        along_y1(k)
    along_y2(2)
    for k in (1, 3):
        along_y2(k)
    x_step2(NC - 1)
    sum_y(2)
    for d in range(2):
        z1(d).start()
    along_y2(0)
    for k in (1, 3):
        sum_y(k)
    x_step3(NC - 2)
    for d in range(2):
        z1(d).wait_recv()
        k = STEP[d]
        zs[k, d] = (zs[k, d].astype(F32) + gz1[d].astype(F32)).astype(BF16)
        z2(d).start()
    sum_y(0)
    x_step3(NC - 1)
    for d in range(2):
        z2(d).wait_recv()
    total = zs[0].astype(F32) + gz2[0].astype(F32) + gz2[1].astype(F32)
    for h in range(2):
        ng_out[:, h * HALF:(h + 1) * HALF] = total[h].astype(BF16)

    for d in range(2):
        for r in range(2):
            for a in range(2):
                az(d, a, r).wait_send()
            azf(d, r).wait_send()
            for k in range(4):
                for a in range(2):
                    ay(k, d, a, r).wait_send()
                ayf(k, d, r).wait_send()
        for k in range(4):
            y1(k, d).wait_send()
            y2(k, d).wait_send()
        z1(d).wait_send()
        z2(d).wait_send()

    def sent(j, carry):
        core_copy(j).wait_send()
        for side in range(2):
            here = place(side)
            for a in range(2):
                @pl.when(here == NEAR)
                def _():
                    near(j, side, a).wait_send()

                @pl.when(here >= RELAY)
                def _():
                    chain(j, side, a).wait_send()

                @pl.when(here == OWNER)
                def _():
                    spread_near(j, side, a).wait_send()

                @pl.when((here == OWNER) | (here == RELAY))
                def _():
                    spread(j, side, a).wait_send()

            core_share(j, side).wait_send()
            x1(j, side).wait_send()
            x2(j, side).wait_send()
        return carry

    lax.fori_loop(0, NC, sent, 0)


def write_out(*refs):
    sources, results, sem = refs[:3], refs[3:6], refs[6]
    copies = [pltpu.make_async_copy(s, r, sem.at[n]) for n, (s, r) in enumerate(zip(sources, results))]
    for copy in copies:
        copy.start()
    for copy in copies:
        copy.wait()


def per_device(normed, cotangent, w_in, w_out):
    vmem = pl.BlockSpec(memory_space=pltpu.VMEM)
    hbm = pl.BlockSpec(memory_space=pltpu.HBM)
    two = lambda *shape: [pltpu.SemaphoreType.DMA(shape)] * 2
    ng, win_t, wout = pl.pallas_call(
        kernel,
        out_shape=(
            jax.ShapeDtypeStruct((ROWS, DM), BF16),
            jax.ShapeDtypeStruct((FH // 4, DM), F32),
            jax.ShapeDtypeStruct((FH // 4, DM), F32),
        ),
        in_specs=[hbm, hbm, hbm, hbm],
        out_specs=[vmem, vmem, vmem],
        scratch_shapes=[
            pltpu.VMEM((2, TOK, DM), BF16),
            pltpu.VMEM((DM, FH), BF16),
            pltpu.VMEM((NC, 4, Q, DM), BF16),
            pltpu.VMEM((NC, 4, Q, DM), BF16),
            pltpu.VMEM((NC, 2, 2, 2, Q, TOK), BF16),
            pltpu.VMEM((NC, 2, 2, Q, TOK), BF16),
            pltpu.VMEM((NC, 2, 2, 2, Q, TOK), BF16),
            pltpu.VMEM((NC, 2, 4, Q, TOK), BF16),
            pltpu.VMEM((NC, 2, 4, Q, DM), BF16),
            pltpu.VMEM((NC, 2, Q, DM), BF16),
            pltpu.VMEM((NC, 2, 2, Q, DM), BF16),
            pltpu.VMEM((TOK, DM), F32),
            pltpu.VMEM((4, 4, 2, ROWS, HALF), BF16),
            pltpu.VMEM((4, 2, ROWS, HALF), BF16),
            pltpu.VMEM((4, 2, 2, ROWS, HALF), BF16),
            pltpu.VMEM((4, 2, ROWS, HALF), BF16),
            pltpu.VMEM((2, ROWS, HALF), BF16),
            pltpu.VMEM((2, 2, ROWS, HALF), BF16),
            pltpu.SemaphoreType.DMA((7,)),
            *two(2, 2, 2), *two(2, 2), *two(4, 2, 2, 2), *two(4, 2, 2),
            *two(NC), *two(NC, 2, 2), *two(NC, 2, 2), *two(NC, 2, 2), *two(NC, 2, 2), *two(NC, 2), *two(NC, 2), *two(NC, 2),
            *two(4, 2), *two(4, 2), *two(2), *two(2),
        ],
        compiler_params=pltpu.CompilerParams(
            collective_id=0, has_side_effects=True, vmem_limit_bytes=48 * 1024 * 1024
        ),
        name="mlp_branch",
    )(*[pltpu.with_memory_space_constraint(t, pltpu.HBM) for t in (normed, cotangent, w_in, w_out.reshape(4, NC, Q, DM))])
    sums = (ng, win_t, wout)
    ng, win_t, wout = pl.pallas_call(
        write_out,
        out_shape=[jax.ShapeDtypeStruct(s.shape, s.dtype) for s in sums],
        in_specs=[vmem] * 3,
        out_specs=[hbm] * 3,
        scratch_shapes=[pltpu.SemaphoreType.DMA((3,))],
        name="write_out",
    )(*sums)
    return ng, win_t.T, wout


def solution(mesh):
    return jax.shard_map(
        per_device,
        mesh=mesh,
        in_specs=(P(("dp", "mx"), "my"), P(("dp", "mx"), "my"), P("my", "mx"), P("mx", "my")),
        out_specs=(P(("dp", "mx"), "my"), P("my", ("mx", "dp")), P(("mx", "dp"), "my")),
        check_vma=False,
    )
```

```python
import jax
import jax.numpy as jnp
from jax import lax
from jax.experimental import pallas as pl
from jax.experimental.pallas import tpu as pltpu
from jax.sharding import PartitionSpec as P

MESH = pl.DeviceIdType.MESH
BF16, F32 = jnp.bfloat16, jnp.float32

NC = 3
ROWS = 32
PIECE = ROWS // 2
GROUP = 4 * ROWS
TOK = 4 * GROUP
DM = 768
FH = 768
FC = FH // NC
Q = FC // 4
HALF = DM // 2

K_OF_P = (0, 3, 1, 2)
P_OF_K = (0, 2, 3, 1)
STEP = (1, 3)

START = (0, 5, 8, 11)
STEPS = START[3] + NC + 5


def nt(a, b):
    return lax.dot_general(a, b, (((1,), (1,)), ((), ())), preferred_element_type=F32)


def nn(a, b):
    return lax.dot_general(a, b, (((1,), (0,)), ((), ())), preferred_element_type=F32)


def tn(a, b):
    return lax.dot_general(a, b, (((0,), (0,)), ((), ())), preferred_element_type=F32)


def activate(preact, upstream):
    cumulative = 0.5 * (1.0 + lax.erf(preact * 0.7071067811865476))
    density = jnp.exp(-0.5 * preact * preact) * 0.3989422804014327
    activation = (preact * cumulative).astype(BF16)
    hidden_grad = (upstream * (cumulative + preact * density)).astype(BF16)
    return activation, hidden_grad


def kernel(
    normed, cotangent, w_in, w_out,
    ng_out, win_out, wout_out,
    xg, win_v, w1t, wo, pu, crecv, zrecv, ah, dw, xr1, xr2, ngb, yr1, yr2, zs, gz1, gz2,
    lsem, az_s, az_r, azf_s, azf_r, ay_s, ay_r, ayf_s, ayf_r,
    co_s, co_r, ne_s, ne_r, ch_s, ch_r, sn_s, sn_r, sp_s, sp_r, ce_s, ce_r, x1_s, x1_r, x2_s, x2_r,
    gy1_s, gy1_r, gy2_s, gy2_r, gz1_s, gz1_r, gz2_s, gz2_r,
):
    x = lax.axis_index("dp")
    mx = lax.axis_index("mx")
    my = lax.axis_index("my")
    zh, y = mx // 4, mx % 4
    zl, c = my // 2, my % 2
    o = 1 - c

    def at_x(k):
        return {"dp": (x + k) % 4}

    def at_y(k):
        return {"mx": zh * 4 + (y + k) % 4}

    def at_zh(k):
        return {"mx": ((zh + k) % 4) * 4 + y}

    def at_zl(k):
        return {"my": ((zl + k) % 4) * 2 + c}

    at_core = {"my": zl * 2 + o}

    def rc(src, dst, send, recv, device):
        return pltpu.make_async_remote_copy(
            src_ref=src, dst_ref=dst, send_sem=send, recv_sem=recv, device_id=device, device_id_type=MESH
        )

    load_own = [pltpu.make_async_copy(t, xg.at[a, 0, 0], lsem.at[5 + a]) for a, t in enumerate((normed, cotangent))]
    load_in = pltpu.make_async_copy(w_in, win_v, lsem.at[4])
    load_out = [pltpu.make_async_copy(w_out.at[g], wo.at[:, g], lsem.at[g]) for g in range(4)]
    for copy in (*load_own, load_in, *load_out):
        copy.start()

    barrier = pltpu.get_barrier_semaphore()
    partners = [at_core]
    for k in (1, 3):
        partners += [at_x(k), at_y(k), at_zh(k), at_zl(k)]
    for device in partners:
        pl.semaphore_signal(barrier, inc=1, device_id=device, device_id_type=MESH)
    pl.semaphore_wait(barrier, len(partners))

    def rows(a, p, yy, r):
        return xg.at[a, p, yy, pl.ds(r * PIECE, PIECE)]

    def az(d, a, r):
        there = rows(a, P_OF_K[STEP[1 - d]], 0, r)
        return rc(rows(a, 0, 0, r), there, az_s.at[d, a, r], az_r.at[d, a, r], at_zh(STEP[d]))

    def azf(d, r):
        here = rows(d, P_OF_K[STEP[1 - d]], 0, r)
        return rc(here, rows(d, 3, 0, r), azf_s.at[d, r], azf_r.at[d, r], at_zh(STEP[d]))

    def ay(p, d, a, r):
        there = rows(a, p, STEP[1 - d], r)
        return rc(rows(a, p, 0, r), there, ay_s.at[p, d, a, r], ay_r.at[p, d, a, r], at_y(STEP[d]))

    def ayf(p, d, r):
        here = rows(d, p, STEP[1 - d], r)
        return rc(here, rows(d, p, 2, r), ayf_s.at[p, d, r], ayf_r.at[p, d, r], at_y(STEP[d]))

    def along_y(p, a, r):
        for d in range(2):
            ay(p, d, a, r).start()

    def further_y(p, a, r):
        ay(p, a, a, r).wait_recv()
        ayf(p, a, r).start()

    def group_here(p):
        for d in range(2):
            for r in range(2):
                ay(p, d, 1 - d, r).wait_recv()
                ayf(p, d, r).wait_recv()

    for copy in load_own:
        copy.wait()
    for a in range(2):
        for r in range(2):
            az(0, a, r).start()
            az(1, 1 - a, r).start()
            ay(0, 0, a, r).start()
            ay(0, 1, 1 - a, r).start()

    load_in.wait()
    for k in range(FH // 128):
        turned = win_v[:, k * 128:(k + 1) * 128].T
        for u in range(0, 128, 32):
            g, rest = divmod(k * 128 + u, FH // 4)
            w1t[rest // Q, g, pl.ds(rest % Q, 32)] = turned[u:u + 32]
    for copy in load_out:
        copy.wait()

    for r in range(2):
        for a in range(2):
            further_y(0, a, r)

    WAVES = [[(0, 0, r), (1, 1, r)] for r in range(2)] + [[(0, 1, r), (1, 0, r)] for r in range(2)]

    def wave(w):
        if w < 4:
            for d, a, r in WAVES[w]:
                az(d, a, r).wait_recv()
                if d == a:
                    azf(d, r).start()
                along_y(P_OF_K[STEP[1 - d]], a, r)
        else:
            for d in range(2):
                azf(d, w - 4).wait_recv()
                along_y(3, d, w - 4)

    def wave_on(w):
        if w < 4:
            for d, a, r in WAVES[w]:
                further_y(P_OF_K[STEP[1 - d]], a, r)
        else:
            for d in range(2):
                further_y(3, d, w - 4)

    group_here(0)

    NEAR, OWNER, RELAY, FAR = range(4)

    def place(side):
        return zl if side == 0 else 3 - zl

    def core_copy(j, p):
        return rc(pu.at[j, p, o], crecv.at[j, p], co_s.at[j, p], co_r.at[j, p], at_core)

    def near(j, p, side):
        there = zrecv.at[j, p, side, 0]
        return rc(pu.at[j, p, c, side], there, ne_s.at[j, p, side], ne_r.at[j, p, side], at_zl(STEP[side]))

    def chain(j, p, side):
        there = zrecv.at[j, p, side, 1]
        return rc(pu.at[j, p, c, side], there, ch_s.at[j, p, side], ch_r.at[j, p, side], at_zl(STEP[1 - side]))

    def spread_near(j, p, side):
        here = ah.at[:, j, p, 2 * c + side]
        return rc(here, here, sn_s.at[j, p, side], sn_r.at[j, p, side], at_zl(STEP[1 - side]))

    def spread(j, p, side):
        here = ah.at[:, j, p, 2 * c + side]
        return rc(here, here, sp_s.at[j, p, side], sp_r.at[j, p, side], at_zl(STEP[side]))

    def core_share(j, p, side):
        here = ah.at[:, j, p, 2 * c + side]
        return rc(here, here, ce_s.at[j, p, side], ce_r.at[j, p, side], at_core)

    def core_share_wait(j, p, side):
        here = ah.at[:, j, p, 2 * o + side]
        rc(here, here, ce_s.at[j, p, side], ce_r.at[j, p, side], at_core).wait_recv()

    def x1(j, d):
        return rc(dw.at[j, d, (x + 2) % 4], xr1.at[j, d], x1_s.at[j, d], x1_r.at[j, d], at_x(STEP[d]))

    def x2(j, d):
        return rc(dw.at[j, :, (x + STEP[d]) % 4], xr2.at[j, d], x2_s.at[j, d], x2_r.at[j, d], at_x(STEP[d]))

    def y1(p, d):
        return rc(ngb.at[p, 2, d], yr1.at[p, d], gy1_s.at[p, d], gy1_r.at[p, d], at_y(STEP[d]))

    def y2(p, d):
        return rc(ngb.at[p, STEP[d]], yr2.at[p, d], gy2_s.at[p, d], gy2_r.at[p, d], at_y(STEP[d]))

    def z1(d):
        return rc(zs.at[3, d], gz1.at[d], gz1_s.at[d], gz1_r.at[d], at_zh(STEP[d]))

    def z2(d):
        return rc(zs.at[P_OF_K[STEP[d]]], gz2.at[d], gz2_s.at[d], gz2_r.at[d], at_zh(STEP[d]))

    def forward(j, p):
        for a, w in enumerate((w1t, wo)):
            part = nt(w[j].reshape(FC, DM), xg[a, p].reshape(GROUP, DM)).astype(BF16)
            for q in range(4):
                pu[j, p, q // 2, q % 2, a] = part[q * Q:(q + 1) * Q]
        core_copy(j, p).start()

    def add_core(j, p):
        core_copy(j, p).wait_recv()
        pu[j, p, c] = (pu[j, p, c].astype(F32) + crecv[j, p].astype(F32)).astype(BF16)
        for side in range(2):
            @pl.when(place(side) == FAR)
            def _():
                chain(j, p, side).start()
                near(j, p, 1 - side).start()

    def pass_on(j, p, side):
        chain(j, p, side).wait_recv()
        pu[j, p, c, side] = (pu[j, p, c, side].astype(F32) + zrecv[j, p, side, 1].astype(F32)).astype(BF16)
        chain(j, p, side).start()

    def finish(j, p, side):
        near(j, p, side).wait_recv()
        chain(j, p, side).wait_recv()
        total = pu[j, p, c, side].astype(F32) + zrecv[j, p, side, 0].astype(F32) + zrecv[j, p, side, 1].astype(F32)
        for a, value in enumerate(activate(total[0], total[1])):
            ah[a, j, p, 2 * c + side] = value
        spread(j, p, side).start()
        spread_near(j, p, side).start()
        core_share(j, p, side).start()

    def pass_back(j, p, side):
        spread(j, p, side).wait_recv()
        spread(j, p, side).start()
        core_share(j, p, side).start()

    def take_far(j, p, side):
        spread(j, p, side).wait_recv()
        core_share(j, p, side).start()

    def take_near(j, p, side):
        spread_near(j, p, side).wait_recv()
        core_share(j, p, side).start()

    def units(a, j):
        return jnp.concatenate([ah[a, j, p].reshape(FC, GROUP) for p in range(4)], axis=1)

    def backward(j, p):
        for side in range(2):
            core_share_wait(j, p, side)

        @pl.when(p == 3)
        def _():
            for d in range(2):
                dw[j, d] = nn(units(1 - d, j), xg[d].reshape(TOK, DM)).astype(BF16).reshape(4, Q, DM)
                x1(j, d).start()

        @pl.when(j == NC - 1)
        def _():
            total = tn(ah[1, :, p].reshape(FH, GROUP), w1t[...].reshape(FH, DM)).astype(BF16)
            for h in range(2):
                ngb[p, :, h] = total[:, h * HALF:(h + 1) * HALF].reshape(4, ROWS, HALF)
            for d in range(2):
                y1(p, d).start()

    def x_step2(j):
        for d in range(2):
            x1(j, d).wait_recv()
            to = (x + STEP[d]) % 4
            dw[j, d, to] = (dw[j, d, to].astype(F32) + xr1[j, d].astype(F32)).astype(BF16)
            x2(j, d).start()

    def x_step3(j):
        for d in range(2):
            x2(j, d).wait_recv()
        for a, out in enumerate((win_out, wout_out)):
            out[j * Q:(j + 1) * Q] = dw[j, a, x].astype(F32) + xr2[j, 0, a].astype(F32) + xr2[j, 1, a].astype(F32)

    def along_y2(p):
        for d in range(2):
            y1(p, d).wait_recv()
            ngb[p, STEP[d], d] = (ngb[p, STEP[d], d].astype(F32) + yr1[p, d].astype(F32)).astype(BF16)
            y2(p, d).start()

    def sum_y(p):
        for d in range(2):
            y2(p, d).wait_recv()
        zs[p] = (ngb[p, 0].astype(F32) + yr2[p, 0].astype(F32) + yr2[p, 1].astype(F32)).astype(BF16)

    AHEAD = {0: [0, 1], 1: [2], 2: [3], 3: [4], 4: [5]}
    AFTER = {0: [0], 1: [1], 2: [2], 3: [3], 4: [4], 5: [5]}

    def step(tau, carry):
        def stage(s, run, on=None):
            slot = tau - s
            p = sum(jnp.where(slot >= START[i], 1, 0) for i in range(1, 4))
            first = sum(jnp.where(slot >= START[i], START[i] - START[i - 1], 0) for i in range(1, 4))
            j = slot - first
            here = (slot >= 0) & (j < NC)
            if on is not None:
                here = here & (place(on[0]) == on[1])

            @pl.when(here)
            def _():
                run(j, p)

        def at(n, run):
            @pl.when(tau == n)
            def _():
                run()

        for n, waves in AHEAD.items():
            at(n, lambda: [wave(w) for w in waves])
        for side in range(2):
            stage(5, lambda j, p: take_far(j, p, side), (side, FAR))
            stage(4, lambda j, p: pass_back(j, p, side), (side, RELAY))
            stage(4, lambda j, p: take_near(j, p, side), (side, NEAR))
        for side in range(2):
            stage(3, lambda j, p: finish(j, p, side), (side, OWNER))
        for side in range(2):
            stage(2, lambda j, p: pass_on(j, p, side), (side, RELAY))
        stage(1, add_core)
        for n, waves in AFTER.items():
            at(n, lambda: [wave_on(w) for w in waves])
        for p in range(1, 4):
            at(START[p], lambda: group_here(p))
        stage(0, forward)
        stage(5, backward)
        for p in range(3):
            at(START[p] + NC - 1 + 7, lambda: along_y2(p))
            at(START[p] + NC - 1 + 9, lambda: sum_y(p))
        return carry

    lax.fori_loop(0, STEPS, step, 0)

    x_step2(0)
    for p in range(3):
        if START[p] + NC - 1 + 7 >= STEPS:
            along_y2(p)
    x_step2(1)
    along_y2(3)
    for j in range(2, NC):
        x_step2(j)
    for p in range(3):
        if START[p] + NC - 1 + 9 >= STEPS:
            sum_y(p)
    sum_y(3)
    for d in range(2):
        z1(d).start()
    for j in range(NC - 2):
        x_step3(j)
    for d in range(2):
        z1(d).wait_recv()
        p = P_OF_K[STEP[d]]
        zs[p, d] = (zs[p, d].astype(F32) + gz1[d].astype(F32)).astype(BF16)
        z2(d).start()
    x_step3(NC - 2)
    for d in range(2):
        z2(d).wait_recv()
    total = zs[0].astype(F32) + gz2[0].astype(F32) + gz2[1].astype(F32)
    for h in range(2):
        ng_out[:, h * HALF:(h + 1) * HALF] = total[h].astype(BF16)
    x_step3(NC - 1)

    for d in range(2):
        for r in range(2):
            for a in range(2):
                az(d, a, r).wait_send()
            azf(d, r).wait_send()
            for p in range(4):
                for a in range(2):
                    ay(p, d, a, r).wait_send()
                ayf(p, d, r).wait_send()
        for p in range(4):
            y1(p, d).wait_send()
            y2(p, d).wait_send()
        for j in range(NC):
            x1(j, d).wait_send()
            x2(j, d).wait_send()
        z1(d).wait_send()
        z2(d).wait_send()

    def sent(u, carry):
        j, p = u % NC, u // NC
        core_copy(j, p).wait_send()
        for side in range(2):
            here = place(side)

            @pl.when(here == NEAR)
            def _():
                near(j, p, side).wait_send()

            @pl.when(here >= RELAY)
            def _():
                chain(j, p, side).wait_send()

            @pl.when(here == OWNER)
            def _():
                spread_near(j, p, side).wait_send()

            @pl.when((here == OWNER) | (here == RELAY))
            def _():
                spread(j, p, side).wait_send()

            core_share(j, p, side).wait_send()
        return carry

    lax.fori_loop(0, 4 * NC, sent, 0)


def per_device(normed, cotangent, w_in, w_out):
    vmem = pl.BlockSpec(memory_space=pltpu.VMEM)
    hbm = pl.BlockSpec(memory_space=pltpu.HBM)
    two = lambda *shape: [pltpu.SemaphoreType.DMA(shape)] * 2
    inputs = (normed, cotangent, w_in, w_out.reshape(4, NC, Q, DM))
    ng, win_t, wout = pl.pallas_call(
        kernel,
        out_shape=(
            jax.ShapeDtypeStruct((ROWS, DM), BF16),
            jax.ShapeDtypeStruct((FH // 4, DM), F32),
            jax.ShapeDtypeStruct((FH // 4, DM), F32),
        ),
        in_specs=[hbm, hbm, hbm, hbm],
        out_specs=[vmem, vmem, vmem],
        scratch_shapes=[
            pltpu.VMEM((2, 4, 4, ROWS, DM), BF16),
            pltpu.VMEM((DM, FH), BF16),
            pltpu.VMEM((NC, 4, Q, DM), BF16),
            pltpu.VMEM((NC, 4, Q, DM), BF16),
            pltpu.VMEM((NC, 4, 2, 2, 2, Q, GROUP), BF16),
            pltpu.VMEM((NC, 4, 2, 2, Q, GROUP), BF16),
            pltpu.VMEM((NC, 4, 2, 2, 2, Q, GROUP), BF16),
            pltpu.VMEM((2, NC, 4, 4, Q, GROUP), BF16),
            pltpu.VMEM((NC, 2, 4, Q, DM), BF16),
            pltpu.VMEM((NC, 2, Q, DM), BF16),
            pltpu.VMEM((NC, 2, 2, Q, DM), BF16),
            pltpu.VMEM((4, 4, 2, ROWS, HALF), BF16),
            pltpu.VMEM((4, 2, ROWS, HALF), BF16),
            pltpu.VMEM((4, 2, 2, ROWS, HALF), BF16),
            pltpu.VMEM((4, 2, ROWS, HALF), BF16),
            pltpu.VMEM((2, ROWS, HALF), BF16),
            pltpu.VMEM((2, 2, ROWS, HALF), BF16),
            pltpu.SemaphoreType.DMA((7,)),
            *two(2, 2, 2), *two(2, 2), *two(4, 2, 2, 2), *two(4, 2, 2),
            *two(NC, 4), *two(NC, 4, 2), *two(NC, 4, 2), *two(NC, 4, 2), *two(NC, 4, 2), *two(NC, 4, 2),
            *two(NC, 2), *two(NC, 2),
            *two(4, 2), *two(4, 2), *two(2), *two(2),
        ],
        compiler_params=pltpu.CompilerParams(
            collective_id=0, has_side_effects=True, vmem_limit_bytes=48 * 1024 * 1024
        ),
        name="mlp_branch",
    )(*[pltpu.with_memory_space_constraint(t, pltpu.HBM) for t in inputs])
    return ng, win_t.T, wout


def solution(mesh):
    return jax.shard_map(
        per_device,
        mesh=mesh,
        in_specs=(P(("dp", "mx"), "my"), P(("dp", "mx"), "my"), P("my", "mx"), P("mx", "my")),
        out_specs=(P(("dp", "mx"), "my"), P("my", ("mx", "dp")), P(("mx", "dp"), "my")),
        check_vma=False,
    )
```

```python
import jax
import jax.numpy as jnp
from jax import lax
from jax.experimental import pallas as pl
from jax.experimental.pallas import tpu as pltpu
from jax.sharding import PartitionSpec as P

MESH = pl.DeviceIdType.MESH
BF16, F32 = jnp.bfloat16, jnp.float32

NC = 3
ROWS = 32
PIECE = ROWS // 2
GROUP = 4 * ROWS
TOK = 4 * GROUP
DM = 768
FH = 768
FC = FH // NC
Q = FC // 4
HALF = DM // 2

K_OF_P = (0, 3, 1, 2)
P_OF_K = (0, 2, 3, 1)
STEP = (1, 3)

UNITS = ((0, 0), (0, 1), (0, 2), (1, 0), (2, 0), (1, 1), (3, 0), (3, 1), (3, 2), (2, 1), (1, 2), (2, 2))
GROUP_CODE = sum(p << (2 * n) for n, (p, j) in enumerate(UNITS))
CHUNK_CODE = sum(j << (2 * n) for n, (p, j) in enumerate(UNITS))
GROUP_FIRST = [min(n for n, u in enumerate(UNITS) if u[0] == p) for p in range(4)]
GROUP_LAST = [max(n for n, u in enumerate(UNITS) if u[0] == p) for p in range(4)]
CHUNK_LAST = [max(n for n, u in enumerate(UNITS) if u[1] == j) for j in range(NC)]

SP = 3
S_ADD, S_RELAY, S_FINISH, S_BACK, S_FAR = 1, 1 + SP, 1 + 2 * SP, 1 + 3 * SP, 1 + 4 * SP
S_BWD = S_FAR + 1
STEPS = len(UNITS) + S_BWD
X_STEP2 = 3
Y_STEP2, Y_SUM = 2, 5


def nt(a, b):
    return lax.dot_general(a, b, (((1,), (1,)), ((), ())), preferred_element_type=F32)


def nn(a, b):
    return lax.dot_general(a, b, (((1,), (0,)), ((), ())), preferred_element_type=F32)


def tn(a, b):
    return lax.dot_general(a, b, (((0,), (0,)), ((), ())), preferred_element_type=F32)


def activate(preact, upstream):
    cumulative = 0.5 * (1.0 + lax.erf(preact * 0.7071067811865476))
    density = jnp.exp(-0.5 * preact * preact) * 0.3989422804014327
    activation = (preact * cumulative).astype(BF16)
    hidden_grad = (upstream * (cumulative + preact * density)).astype(BF16)
    return activation, hidden_grad


def kernel(
    normed, cotangent, w_in, w_out,
    ng_out, win_out, wout_out,
    xg, win_v, w1t, wo, pu, crecv, zrecv, ah, dw, xr1, xr2, ngb, yr1, yr2, zs, gz1, gz2,
    lsem, az_s, az_r, azf_s, azf_r, ay_s, ay_r, ayf_s, ayf_r,
    co_s, co_r, ne_s, ne_r, ch_s, ch_r, sn_s, sn_r, sp_s, sp_r, ce_s, ce_r, x1_s, x1_r, x2_s, x2_r,
    gy1_s, gy1_r, gy2_s, gy2_r, gz1_s, gz1_r, gz2_s, gz2_r,
):
    x = lax.axis_index("dp")
    mx = lax.axis_index("mx")
    my = lax.axis_index("my")
    zh, y = mx // 4, mx % 4
    zl, c = my // 2, my % 2

    def at_x(k):
        return {"dp": (x + k) % 4}

    def at_y(k):
        return {"mx": zh * 4 + (y + k) % 4}

    def at_zh(k):
        return {"mx": ((zh + k) % 4) * 4 + y}

    def at_zl(k):
        return {"my": ((zl + k) % 4) * 2 + c}

    at_core = {"my": zl * 2 + 1 - c}

    def rc(src, dst, send, recv, device):
        return pltpu.make_async_remote_copy(
            src_ref=src, dst_ref=dst, send_sem=send, recv_sem=recv, device_id=device, device_id_type=MESH
        )

    load_own = [pltpu.make_async_copy(t, xg.at[a, 0, 0], lsem.at[5 + a]) for a, t in enumerate((normed, cotangent))]
    load_in = pltpu.make_async_copy(w_in, win_v, lsem.at[4])
    load_out = [pltpu.make_async_copy(w_out.at[g], wo.at[:, g], lsem.at[g]) for g in range(4)]
    for copy in (*load_own, load_in, *load_out):
        copy.start()

    barrier = pltpu.get_barrier_semaphore()
    partners = [at_core]
    for k in (1, 3):
        partners += [at_x(k), at_y(k), at_zh(k), at_zl(k)]
    for device in partners:
        pl.semaphore_signal(barrier, inc=1, device_id=device, device_id_type=MESH)
    pl.semaphore_wait(barrier, len(partners))

    def rows(a, p, yy, r):
        return xg.at[a, p, yy, pl.ds(r * PIECE, PIECE)]

    def az(d, a, r):
        there = rows(a, P_OF_K[STEP[1 - d]], 0, r)
        return rc(rows(a, 0, 0, r), there, az_s.at[d, a, r], az_r.at[d, a, r], at_zh(STEP[d]))

    def azf(d, r):
        here = rows(d, P_OF_K[STEP[1 - d]], 0, r)
        return rc(here, rows(d, 3, 0, r), azf_s.at[d, r], azf_r.at[d, r], at_zh(STEP[d]))

    def ay(p, d, a, r):
        there = rows(a, p, STEP[1 - d], r)
        return rc(rows(a, p, 0, r), there, ay_s.at[p, d, a, r], ay_r.at[p, d, a, r], at_y(STEP[d]))

    def ayf(p, d, r):
        here = rows(d, p, STEP[1 - d], r)
        return rc(here, rows(d, p, 2, r), ayf_s.at[p, d, r], ayf_r.at[p, d, r], at_y(STEP[d]))

    def along_y(p, a, r):
        for d in range(2):
            ay(p, d, a, r).start()

    def further_y(p, a, r):
        ay(p, a, a, r).wait_recv()
        ayf(p, a, r).start()

    def group_here(p):
        for d in range(2):
            for r in range(2):
                ay(p, d, 1 - d, r).wait_recv()
                ayf(p, d, r).wait_recv()

    for copy in load_own:
        copy.wait()
    for a in range(2):
        for r in range(2):
            az(0, a, r).start()
            az(1, 1 - a, r).start()
            ay(0, 0, a, r).start()
            ay(0, 1, 1 - a, r).start()

    load_in.wait()
    for k in range(FH // 128):
        turned = win_v[:, k * 128:(k + 1) * 128].T
        for u in range(0, 128, 32):
            g, rest = divmod(k * 128 + u, FH // 4)
            w1t[rest // Q, g, pl.ds(rest % Q, 32)] = turned[u:u + 32]
    for copy in load_out:
        copy.wait()

    WAVES = [[(0, 0, r), (1, 1, r)] for r in range(2)] + [[(0, 1, r), (1, 0, r)] for r in range(2)]

    def wave(w):
        if w < 4:
            for d, a, r in WAVES[w]:
                az(d, a, r).wait_recv()
                if d == a:
                    azf(d, r).start()
                along_y(P_OF_K[STEP[1 - d]], a, r)
        else:
            for d in range(2):
                azf(d, w - 4).wait_recv()
                along_y(3, d, w - 4)

    def wave_on(w):
        if w < 4:
            for d, a, r in WAVES[w]:
                further_y(P_OF_K[STEP[1 - d]], a, r)
        else:
            for d in range(2):
                further_y(3, d, w - 4)

    for r in range(2):
        for a in range(2):
            further_y(0, a, r)
    wave(0)
    wave(1)
    wave(2)
    wave_on(0)
    group_here(0)
    wave(3)
    wave_on(1)
    wave(4)
    wave_on(2)
    wave(5)
    wave_on(3)

    NEAR, OWNER, RELAY, FAR = range(4)

    def place(side):
        return zl if side == 0 else 3 - zl

    def core_copy(j, p):
        return rc(pu.at[j, p], crecv.at[j, p], co_s.at[j, p], co_r.at[j, p], at_core)

    def near(j, p, side):
        there = zrecv.at[j, p, side, 0]
        return rc(pu.at[j, p, side], there, ne_s.at[j, p, side], ne_r.at[j, p, side], at_zl(STEP[side]))

    def chain(j, p, side):
        there = zrecv.at[j, p, side, 1]
        return rc(pu.at[j, p, side], there, ch_s.at[j, p, side], ch_r.at[j, p, side], at_zl(STEP[1 - side]))

    def spread_near(j, p, side):
        here = ah.at[:, j, p, side]
        return rc(here, here, sn_s.at[j, p, side], sn_r.at[j, p, side], at_zl(STEP[1 - side]))

    def spread(j, p, side):
        here = ah.at[:, j, p, side]
        return rc(here, here, sp_s.at[j, p, side], sp_r.at[j, p, side], at_zl(STEP[side]))

    def core_share(j, p, side):
        here = ah.at[:, j, p, side]
        return rc(here, here, ce_s.at[j, p, side], ce_r.at[j, p, side], at_core)

    def x1(j, d):
        return rc(dw.at[j, d, (x + 2) % 4], xr1.at[j, d], x1_s.at[j, d], x1_r.at[j, d], at_x(STEP[d]))

    def x2(j, d):
        return rc(dw.at[j, :, (x + STEP[d]) % 4], xr2.at[j, d], x2_s.at[j, d], x2_r.at[j, d], at_x(STEP[d]))

    def y1(p, d):
        return rc(ngb.at[p, 2, d], yr1.at[p, d], gy1_s.at[p, d], gy1_r.at[p, d], at_y(STEP[d]))

    def y2(p, d):
        return rc(ngb.at[p, STEP[d]], yr2.at[p, d], gy2_s.at[p, d], gy2_r.at[p, d], at_y(STEP[d]))

    def z1(d):
        return rc(zs.at[3, d], gz1.at[d], gz1_s.at[d], gz1_r.at[d], at_zh(STEP[d]))

    def z2(d):
        return rc(zs.at[P_OF_K[STEP[d]]], gz2.at[d], gz2_s.at[d], gz2_r.at[d], at_zh(STEP[d]))

    def forward(j, p):
        for a, w in enumerate((w1t, wo)):
            part = nt(w[j].reshape(FC, DM), xg[a, p].reshape(GROUP, DM)).astype(BF16)
            for side in range(2):
                pu[j, p, side, a] = part[side * 2 * Q:(side + 1) * 2 * Q]

        @pl.when(c == 0)
        def _():
            core_copy(j, p).start()

    def add_core(j, p):
        core_copy(j, p).wait_recv()
        pu[j, p] = (pu[j, p].astype(F32) + crecv[j, p].astype(F32)).astype(BF16)
        for side in range(2):
            @pl.when(place(side) == FAR)
            def _():
                chain(j, p, side).start()
                near(j, p, 1 - side).start()

    def pass_on(j, p, side):
        chain(j, p, side).wait_recv()
        pu[j, p, side] = (pu[j, p, side].astype(F32) + zrecv[j, p, side, 1].astype(F32)).astype(BF16)
        chain(j, p, side).start()

    def finish(j, p, side):
        near(j, p, side).wait_recv()
        chain(j, p, side).wait_recv()
        total = pu[j, p, side].astype(F32) + zrecv[j, p, side, 0].astype(F32) + zrecv[j, p, side, 1].astype(F32)
        for a, value in enumerate(activate(total[0], total[1])):
            ah[a, j, p, side] = value
        spread(j, p, side).start()
        spread_near(j, p, side).start()
        core_share(j, p, side).start()

    def pass_back(j, p, side):
        spread(j, p, side).wait_recv()
        spread(j, p, side).start()
        core_share(j, p, side).start()

    def take_far(j, p, side):
        spread(j, p, side).wait_recv()
        core_share(j, p, side).start()

    def take_near(j, p, side):
        spread_near(j, p, side).wait_recv()
        core_share(j, p, side).start()

    def units(a, j):
        return jnp.concatenate([ah[a, j, p].reshape(FC, GROUP) for p in range(4)], axis=1)

    def take_shares(j, p):
        for side in range(2):
            core_share(j, p, side).wait_recv()

    def weight_grads(j, p):
        for d in range(2):
            dw[j, d] = nn(units(1 - d, j), xg[d].reshape(TOK, DM)).astype(BF16).reshape(4, Q, DM)
            x1(j, d).start()

    def normed_grad(j, p):
        total = tn(ah[1, :, p].reshape(FH, GROUP), w1t[...].reshape(FH, DM)).astype(BF16)
        for h in range(2):
            ngb[p, :, h] = total[:, h * HALF:(h + 1) * HALF].reshape(4, ROWS, HALF)
        for d in range(2):
            y1(p, d).start()

    def x_step2(j):
        for d in range(2):
            x1(j, d).wait_recv()
            to = (x + STEP[d]) % 4
            dw[j, d, to] = (dw[j, d, to].astype(F32) + xr1[j, d].astype(F32)).astype(BF16)
            x2(j, d).start()

    def x_step3(j):
        for d in range(2):
            x2(j, d).wait_recv()
        for a, out in enumerate((win_out, wout_out)):
            out[j * Q:(j + 1) * Q] = dw[j, a, x].astype(F32) + xr2[j, 0, a].astype(F32) + xr2[j, 1, a].astype(F32)

    def along_y2(p):
        for d in range(2):
            y1(p, d).wait_recv()
            ngb[p, STEP[d], d] = (ngb[p, STEP[d], d].astype(F32) + yr1[p, d].astype(F32)).astype(BF16)
            y2(p, d).start()

    def sum_y(p):
        for d in range(2):
            y2(p, d).wait_recv()
        zs[p] = (ngb[p, 0].astype(F32) + yr2[p, 0].astype(F32) + yr2[p, 1].astype(F32)).astype(BF16)

    AFTER = {1: lambda: wave_on(4), 2: lambda: wave_on(5)}

    def step(tau, carry):
        def stage(s, run, on=None, core=None, among=None):
            slot = tau - s
            here = (slot >= 0) & (slot < len(UNITS))
            if on is not None:
                here = here & (c == 1) & (place(on[0]) == on[1])
            if core is not None:
                here = here & (c == core)
            if among is not None:
                here = sum(jnp.where(slot == n, 1, 0) for n in among) > 0

            @pl.when(here)
            def _():
                j, p = ((code >> (2 * slot)) & 3 for code in (CHUNK_CODE, GROUP_CODE))
                run(j, p)

        def at(n, run):
            @pl.when(tau == n)
            def _():
                run()

        for side in range(2):
            stage(S_FAR, lambda j, p: take_far(j, p, side), (side, FAR))
            stage(S_BACK, lambda j, p: pass_back(j, p, side), (side, RELAY))
            stage(S_BACK, lambda j, p: take_near(j, p, side), (side, NEAR))
        for side in range(2):
            stage(S_FINISH, lambda j, p: finish(j, p, side), (side, OWNER))
        for side in range(2):
            stage(S_RELAY, lambda j, p: pass_on(j, p, side), (side, RELAY))
        stage(S_ADD, add_core, core=1)
        for n, run in AFTER.items():
            at(n, run)
        for p in range(1, 4):
            at(GROUP_FIRST[p], lambda: group_here(p))
        stage(0, forward)
        stage(S_BWD, take_shares, core=0)
        stage(S_BWD, weight_grads, among=CHUNK_LAST)
        stage(S_BWD, normed_grad, among=GROUP_LAST)
        for j in range(NC):
            at(CHUNK_LAST[j] + S_BWD + X_STEP2, lambda: x_step2(j))
        for p in range(4):
            at(GROUP_LAST[p] + S_BWD + Y_STEP2, lambda: along_y2(p))
            at(GROUP_LAST[p] + S_BWD + Y_SUM, lambda: sum_y(p))
        return carry

    lax.fori_loop(0, STEPS, step, 0)

    def rest_x(j):
        if CHUNK_LAST[j] + S_BWD + X_STEP2 >= STEPS:
            x_step2(j)

    def rest_y2(p):
        if GROUP_LAST[p] + S_BWD + Y_STEP2 >= STEPS:
            along_y2(p)

    def rest_y(p):
        if GROUP_LAST[p] + S_BWD + Y_SUM >= STEPS:
            sum_y(p)

    rest_y2(3)
    rest_y(0)
    rest_x(0)
    rest_y(3)
    for d in range(2):
        z1(d).start()
    rest_y2(1)
    rest_y2(2)
    rest_x(1)
    x_step3(0)
    rest_y(1)
    rest_x(2)
    rest_y(2)
    for d in range(2):
        z1(d).wait_recv()
        p = P_OF_K[STEP[d]]
        zs[p, d] = (zs[p, d].astype(F32) + gz1[d].astype(F32)).astype(BF16)
        z2(d).start()
    x_step3(1)
    for d in range(2):
        z2(d).wait_recv()
    total = zs[0].astype(F32) + gz2[0].astype(F32) + gz2[1].astype(F32)
    for h in range(2):
        ng_out[:, h * HALF:(h + 1) * HALF] = total[h].astype(BF16)
    x_step3(2)

    for d in range(2):
        for r in range(2):
            for a in range(2):
                az(d, a, r).wait_send()
            azf(d, r).wait_send()
            for p in range(4):
                for a in range(2):
                    ay(p, d, a, r).wait_send()
                ayf(p, d, r).wait_send()
        for p in range(4):
            y1(p, d).wait_send()
            y2(p, d).wait_send()
        for j in range(NC):
            x1(j, d).wait_send()
            x2(j, d).wait_send()
        z1(d).wait_send()
        z2(d).wait_send()

    def sent(u, carry):
        j, p = u % NC, u // NC
        @pl.when(c == 0)
        def _():
            core_copy(j, p).wait_send()

        for side in range(2):
            here = place(side)

            @pl.when((c == 1) & (here == NEAR))
            def _():
                near(j, p, side).wait_send()

            @pl.when((c == 1) & (here >= RELAY))
            def _():
                chain(j, p, side).wait_send()

            @pl.when((c == 1) & (here == OWNER))
            def _():
                spread_near(j, p, side).wait_send()

            @pl.when((c == 1) & ((here == OWNER) | (here == RELAY)))
            def _():
                spread(j, p, side).wait_send()

            @pl.when(c == 1)
            def _():
                core_share(j, p, side).wait_send()
        return carry

    lax.fori_loop(0, 4 * NC, sent, 0)


def per_device(normed, cotangent, w_in, w_out):
    vmem = pl.BlockSpec(memory_space=pltpu.VMEM)
    hbm = pl.BlockSpec(memory_space=pltpu.HBM)
    two = lambda *shape: [pltpu.SemaphoreType.DMA(shape)] * 2
    inputs = (normed, cotangent, w_in, w_out.reshape(4, NC, Q, DM))
    ng, win_t, wout = pl.pallas_call(
        kernel,
        out_shape=(
            jax.ShapeDtypeStruct((ROWS, DM), BF16),
            jax.ShapeDtypeStruct((FH // 4, DM), F32),
            jax.ShapeDtypeStruct((FH // 4, DM), F32),
        ),
        in_specs=[hbm, hbm, hbm, hbm],
        out_specs=[vmem, vmem, vmem],
        scratch_shapes=[
            pltpu.VMEM((2, 4, 4, ROWS, DM), BF16),
            pltpu.VMEM((DM, FH), BF16),
            pltpu.VMEM((NC, 4, Q, DM), BF16),
            pltpu.VMEM((NC, 4, Q, DM), BF16),
            pltpu.VMEM((NC, 4, 2, 2, 2 * Q, GROUP), BF16),
            pltpu.VMEM((NC, 4, 2, 2, 2 * Q, GROUP), BF16),
            pltpu.VMEM((NC, 4, 2, 2, 2, 2 * Q, GROUP), BF16),
            pltpu.VMEM((2, NC, 4, 2, 2 * Q, GROUP), BF16),
            pltpu.VMEM((NC, 2, 4, Q, DM), BF16),
            pltpu.VMEM((NC, 2, Q, DM), BF16),
            pltpu.VMEM((NC, 2, 2, Q, DM), BF16),
            pltpu.VMEM((4, 4, 2, ROWS, HALF), BF16),
            pltpu.VMEM((4, 2, ROWS, HALF), BF16),
            pltpu.VMEM((4, 2, 2, ROWS, HALF), BF16),
            pltpu.VMEM((4, 2, ROWS, HALF), BF16),
            pltpu.VMEM((2, ROWS, HALF), BF16),
            pltpu.VMEM((2, 2, ROWS, HALF), BF16),
            pltpu.SemaphoreType.DMA((7,)),
            *two(2, 2, 2), *two(2, 2), *two(4, 2, 2, 2), *two(4, 2, 2),
            *two(NC, 4), *two(NC, 4, 2), *two(NC, 4, 2), *two(NC, 4, 2), *two(NC, 4, 2), *two(NC, 4, 2),
            *two(NC, 2), *two(NC, 2),
            *two(4, 2), *two(4, 2), *two(2), *two(2),
        ],
        compiler_params=pltpu.CompilerParams(
            collective_id=0, has_side_effects=True, vmem_limit_bytes=48 * 1024 * 1024
        ),
        name="mlp_branch",
    )(*[pltpu.with_memory_space_constraint(t, pltpu.HBM) for t in inputs])
    return ng, win_t.T, wout


def solution(mesh):
    return jax.shard_map(
        per_device,
        mesh=mesh,
        in_specs=(P(("dp", "mx"), "my"), P(("dp", "mx"), "my"), P("my", "mx"), P("mx", "my")),
        out_specs=(P(("dp", "mx"), "my"), P("my", ("mx", "dp")), P(("mx", "dp"), "my")),
        check_vma=False,
    )
```

```python
import jax
import jax.numpy as jnp
from jax import lax
from jax.experimental import pallas as pl
from jax.experimental.pallas import tpu as pltpu
from jax.sharding import PartitionSpec as P

MESH = pl.DeviceIdType.MESH
BF16, F32 = jnp.bfloat16, jnp.float32

NC = 3
ROWS = 32
PIECE = ROWS // 2
GROUP = 4 * ROWS
TOK = 4 * GROUP
DM = 768
FH = 768
FC = FH // NC
Q = FC // 4

K_OF_P = (0, 3, 1, 2)
P_OF_K = (0, 2, 3, 1)
STEP = (1, 3, 2)
FROM = (3, 1, 2)

UNITS = ((0, 0), (0, 1), (0, 2), (1, 0), (2, 0), (1, 1), (3, 0), (3, 1), (2, 1), (3, 2), (1, 2), (2, 2))
GROUP_CODE = sum(p << (2 * n) for n, (p, j) in enumerate(UNITS))
CHUNK_CODE = sum(j << (2 * n) for n, (p, j) in enumerate(UNITS))
GROUP_FIRST = [min(n for n, u in enumerate(UNITS) if u[0] == p) for p in range(4)]
GROUP_LAST = [max(n for n, u in enumerate(UNITS) if u[0] == p) for p in range(4)]
CHUNK_LAST = [max(n for n, u in enumerate(UNITS) if u[1] == j) for j in range(NC)]

SP = 3
S_ADD, S_RELAY, S_FINISH, S_BACK, S_FAR = 1, 1 + SP, 1 + 2 * SP, 1 + 3 * SP, 1 + 4 * SP
S_BWD = S_FAR + 1
STEPS = len(UNITS) + S_BWD
X_STEP2 = 3
Y_SUM = 4


def nt(a, b):
    return lax.dot_general(a, b, (((1,), (1,)), ((), ())), preferred_element_type=F32)


def nn(a, b):
    return lax.dot_general(a, b, (((1,), (0,)), ((), ())), preferred_element_type=F32)


def tn(a, b):
    return lax.dot_general(a, b, (((0,), (0,)), ((), ())), preferred_element_type=F32)


def activate(preact, upstream):
    cumulative = 0.5 * (1.0 + lax.erf(preact * 0.7071067811865476))
    density = jnp.exp(-0.5 * preact * preact) * 0.3989422804014327
    activation = (preact * cumulative).astype(BF16)
    hidden_grad = (upstream * (cumulative + preact * density)).astype(BF16)
    return activation, hidden_grad


def kernel(
    normed, cotangent, w_in, w_out,
    ng_out, win_out, wout_out,
    xg, win_v, w1t, wo, pu, crecv, zrecv, ah, dw, xr1, xr2, ngb, yr, zs, zr,
    lsem, az_s, az_r, azf_s, azf_r, ay_s, ay_r,
    co_s, co_r, ne_s, ne_r, ch_s, ch_r, sn_s, sn_r, sp_s, sp_r, ce_s, ce_r, x1_s, x1_r, x2_s, x2_r,
    gy_s, gy_r, gz_s, gz_r,
):
    x = lax.axis_index("dp")
    mx = lax.axis_index("mx")
    my = lax.axis_index("my")
    zh, y = mx // 4, mx % 4
    zl, c = my // 2, my % 2

    def at_x(k):
        return {"dp": (x + k) % 4}

    def at_y(k):
        return {"mx": zh * 4 + (y + k) % 4}

    def at_zh(k):
        return {"mx": ((zh + k) % 4) * 4 + y}

    def at_zl(k):
        return {"my": ((zl + k) % 4) * 2 + c}

    at_core = {"my": zl * 2 + 1 - c}

    def rc(src, dst, send, recv, device):
        return pltpu.make_async_remote_copy(
            src_ref=src, dst_ref=dst, send_sem=send, recv_sem=recv, device_id=device, device_id_type=MESH
        )

    load_own = [pltpu.make_async_copy(t, xg.at[a, 0, 0], lsem.at[5 + a]) for a, t in enumerate((normed, cotangent))]
    load_in = pltpu.make_async_copy(w_in, win_v, lsem.at[4])
    load_out = [pltpu.make_async_copy(w_out.at[g], wo.at[:, g], lsem.at[g]) for g in range(4)]
    for copy in (*load_own, load_in, *load_out):
        copy.start()

    barrier = pltpu.get_barrier_semaphore()
    partners = [at_core, at_y(2), at_zh(2)]
    for k in (1, 3):
        partners += [at_x(k), at_y(k), at_zh(k), at_zl(k)]
    for device in partners:
        pl.semaphore_signal(barrier, inc=1, device_id=device, device_id_type=MESH)
    pl.semaphore_wait(barrier, len(partners))

    def rows(a, p, yy, r):
        return xg.at[a, p, yy, pl.ds(r * PIECE, PIECE)]

    def az(d, a, r):
        there = rows(a, P_OF_K[FROM[d]], 0, r)
        return rc(rows(a, 0, 0, r), there, az_s.at[d, a, r], az_r.at[d, a, r], at_zh(STEP[d]))

    def azf(d, r):
        here = rows(d, P_OF_K[FROM[d]], 0, r)
        return rc(here, rows(d, 3, 0, r), azf_s.at[d, r], azf_r.at[d, r], at_zh(STEP[d]))

    def ay(p, d, a, r):
        there = rows(a, p, FROM[d], r)
        return rc(rows(a, p, 0, r), there, ay_s.at[p, d, a, r], ay_r.at[p, d, a, r], at_y(STEP[d]))

    def along_y(p, a, r):
        for d in (2, 0, 1):
            ay(p, d, a, r).start()

    def group_here(p):
        for d in range(3):
            for a in range(2):
                for r in range(2):
                    ay(p, d, a, r).wait_recv()

    for copy in load_own:
        copy.wait()
    for a in range(2):
        for r in range(2):
            az(0, a, r).start()
            az(1, 1 - a, r).start()
    for a in range(2):
        for r in range(2):
            along_y(0, a, r)

    load_in.wait()
    for k in range(FH // 128):
        turned = win_v[:, k * 128:(k + 1) * 128].T
        for u in range(0, 128, 32):
            g, rest = divmod(k * 128 + u, FH // 4)
            w1t[rest // Q, g, pl.ds(rest % Q, 32)] = turned[u:u + 32]
    for copy in load_out:
        copy.wait()

    WAVES = [[(0, 0, r), (1, 1, r)] for r in range(2)] + [[(0, 1, r), (1, 0, r)] for r in range(2)]

    def wave(w):
        if w < 4:
            for d, a, r in WAVES[w]:
                az(d, a, r).wait_recv()
                if d == a:
                    azf(d, r).start()
                along_y(P_OF_K[FROM[d]], a, r)
        else:
            for d in range(2):
                azf(d, w - 4).wait_recv()
                along_y(3, d, w - 4)

    wave(0)
    wave(1)
    group_here(0)
    wave(2)
    wave(3)

    NEAR, OWNER, RELAY, FAR = range(4)

    def place(side):
        return zl if side == 0 else 3 - zl

    def core_copy(j, p):
        return rc(pu.at[j, p], crecv.at[j, p], co_s.at[j, p], co_r.at[j, p], at_core)

    def near(j, p, side):
        there = zrecv.at[j, p, side, 0]
        return rc(pu.at[j, p, side], there, ne_s.at[j, p, side], ne_r.at[j, p, side], at_zl(STEP[side]))

    def chain(j, p, side):
        there = zrecv.at[j, p, side, 1]
        return rc(pu.at[j, p, side], there, ch_s.at[j, p, side], ch_r.at[j, p, side], at_zl(STEP[1 - side]))

    def spread_near(j, p, side):
        here = ah.at[:, j, p, side]
        return rc(here, here, sn_s.at[j, p, side], sn_r.at[j, p, side], at_zl(STEP[1 - side]))

    def spread(j, p, side):
        here = ah.at[:, j, p, side]
        return rc(here, here, sp_s.at[j, p, side], sp_r.at[j, p, side], at_zl(STEP[side]))

    def core_share(j, p, side):
        here = ah.at[:, j, p, side]
        return rc(here, here, ce_s.at[j, p, side], ce_r.at[j, p, side], at_core)

    def x1(j, d):
        return rc(dw.at[j, d, (x + 2) % 4], xr1.at[j, d], x1_s.at[j, d], x1_r.at[j, d], at_x(STEP[d]))

    def x2(j, d):
        return rc(dw.at[j, :, (x + STEP[d]) % 4], xr2.at[j, d], x2_s.at[j, d], x2_r.at[j, d], at_x(STEP[d]))

    def along_gy(p, d):
        return rc(ngb.at[p, STEP[d]], yr.at[p, d], gy_s.at[p, d], gy_r.at[p, d], at_y(STEP[d]))

    def along_gz(d):
        return rc(zs.at[P_OF_K[STEP[d]]], zr.at[d], gz_s.at[d], gz_r.at[d], at_zh(STEP[d]))

    def forward(j, p):
        for a, w in enumerate((w1t, wo)):
            part = nt(w[j].reshape(FC, DM), xg[a, p].reshape(GROUP, DM)).astype(BF16)
            for side in range(2):
                pu[j, p, side, a] = part[side * 2 * Q:(side + 1) * 2 * Q]

        @pl.when(c == 0)
        def _():
            core_copy(j, p).start()

    def add_core(j, p):
        core_copy(j, p).wait_recv()
        pu[j, p] = (pu[j, p].astype(F32) + crecv[j, p].astype(F32)).astype(BF16)
        for side in range(2):
            @pl.when(place(side) == FAR)
            def _():
                chain(j, p, side).start()
                near(j, p, 1 - side).start()

    def pass_on(j, p, side):
        chain(j, p, side).wait_recv()
        pu[j, p, side] = (pu[j, p, side].astype(F32) + zrecv[j, p, side, 1].astype(F32)).astype(BF16)
        chain(j, p, side).start()

    def finish(j, p, side):
        near(j, p, side).wait_recv()
        chain(j, p, side).wait_recv()
        total = pu[j, p, side].astype(F32) + zrecv[j, p, side, 0].astype(F32) + zrecv[j, p, side, 1].astype(F32)
        for a, value in enumerate(activate(total[0], total[1])):
            ah[a, j, p, side] = value
        spread(j, p, side).start()
        spread_near(j, p, side).start()
        core_share(j, p, side).start()

    def pass_back(j, p, side):
        spread(j, p, side).wait_recv()
        spread(j, p, side).start()
        core_share(j, p, side).start()

    def take_far(j, p, side):
        spread(j, p, side).wait_recv()
        core_share(j, p, side).start()

    def take_near(j, p, side):
        spread_near(j, p, side).wait_recv()
        core_share(j, p, side).start()

    def units(a, j):
        return jnp.concatenate([ah[a, j, p].reshape(FC, GROUP) for p in range(4)], axis=1)

    def take_shares(j, p):
        for side in range(2):
            core_share(j, p, side).wait_recv()

    def weight_grads(j, p):
        for d in range(2):
            dw[j, d] = nn(units(1 - d, j), xg[d].reshape(TOK, DM)).astype(BF16).reshape(4, Q, DM)
            x1(j, d).start()

    def normed_grad(j, p):
        total = tn(ah[1, :, p].reshape(FH, GROUP), w1t[...].reshape(FH, DM)).astype(BF16)
        ngb[p] = total.reshape(4, ROWS, DM)
        for d in (2, 0, 1):
            along_gy(p, d).start()

    def x_step2(j):
        for d in range(2):
            x1(j, d).wait_recv()
            to = (x + STEP[d]) % 4
            dw[j, d, to] = (dw[j, d, to].astype(F32) + xr1[j, d].astype(F32)).astype(BF16)
            x2(j, d).start()

    def x_step3(j):
        for d in range(2):
            x2(j, d).wait_recv()
        for a, out in enumerate((win_out, wout_out)):
            out[j * Q:(j + 1) * Q] = dw[j, a, x].astype(F32) + xr2[j, 0, a].astype(F32) + xr2[j, 1, a].astype(F32)

    def sum_y(p):
        total = ngb[p, 0].astype(F32)
        for d in range(3):
            along_gy(p, d).wait_recv()
            total = total + yr[p, d].astype(F32)
        zs[p] = total.astype(BF16)
        for d in range(3):
            if P_OF_K[STEP[d]] == p:
                along_gz(d).start()

    AHEAD = {1: lambda: wave(4), 2: lambda: wave(5)}

    def step(tau, carry):
        def stage(s, run, on=None, core=None, among=None):
            slot = tau - s
            here = (slot >= 0) & (slot < len(UNITS))
            if on is not None:
                here = here & (c == 1) & (place(on[0]) == on[1])
            if core is not None:
                here = here & (c == core)
            if among is not None:
                here = sum(jnp.where(slot == n, 1, 0) for n in among) > 0

            @pl.when(here)
            def _():
                j, p = ((code >> (2 * slot)) & 3 for code in (CHUNK_CODE, GROUP_CODE))
                run(j, p)

        def at(n, run):
            @pl.when(tau == n)
            def _():
                run()

        for n, run in AHEAD.items():
            at(n, run)
        for side in range(2):
            stage(S_FAR, lambda j, p: take_far(j, p, side), (side, FAR))
            stage(S_BACK, lambda j, p: pass_back(j, p, side), (side, RELAY))
            stage(S_BACK, lambda j, p: take_near(j, p, side), (side, NEAR))
        for side in range(2):
            stage(S_FINISH, lambda j, p: finish(j, p, side), (side, OWNER))
        for side in range(2):
            stage(S_RELAY, lambda j, p: pass_on(j, p, side), (side, RELAY))
        stage(S_ADD, add_core, core=1)
        for p in range(1, 4):
            at(GROUP_FIRST[p], lambda: group_here(p))
        stage(0, forward)
        stage(S_BWD, take_shares, core=0)
        stage(S_BWD, weight_grads, among=CHUNK_LAST)
        stage(S_BWD, normed_grad, among=GROUP_LAST)
        for j in range(NC):
            at(CHUNK_LAST[j] + S_BWD + X_STEP2, lambda: x_step2(j))
        for p in range(4):
            at(GROUP_LAST[p] + S_BWD + Y_SUM, lambda: sum_y(p))
        return carry

    lax.fori_loop(0, STEPS, step, 0)

    def rest_x(j):
        if CHUNK_LAST[j] + S_BWD + X_STEP2 >= STEPS:
            x_step2(j)

    def rest_y(p):
        if GROUP_LAST[p] + S_BWD + Y_SUM >= STEPS:
            sum_y(p)

    rest_y(0)
    rest_y(3)
    rest_x(0)
    rest_x(1)
    rest_y(1)
    rest_y(2)
    rest_x(2)
    x_step3(0)
    x_step3(1)
    total = zs[0].astype(F32)
    for d in (2, 0, 1):
        along_gz(d).wait_recv()
        total = total + zr[d].astype(F32)
    ng_out[...] = total.astype(BF16)
    x_step3(2)

    for d in range(3):
        for p in range(4):
            for a in range(2):
                for r in range(2):
                    ay(p, d, a, r).wait_send()
            along_gy(p, d).wait_send()
        along_gz(d).wait_send()
    for d in range(2):
        for r in range(2):
            for a in range(2):
                az(d, a, r).wait_send()
            azf(d, r).wait_send()
        for j in range(NC):
            x1(j, d).wait_send()
            x2(j, d).wait_send()

    def sent(u, carry):
        j, p = u % NC, u // NC
        @pl.when(c == 0)
        def _():
            core_copy(j, p).wait_send()

        for side in range(2):
            here = place(side)

            @pl.when((c == 1) & (here == NEAR))
            def _():
                near(j, p, side).wait_send()

            @pl.when((c == 1) & (here >= RELAY))
            def _():
                chain(j, p, side).wait_send()

            @pl.when((c == 1) & (here == OWNER))
            def _():
                spread_near(j, p, side).wait_send()

            @pl.when((c == 1) & ((here == OWNER) | (here == RELAY)))
            def _():
                spread(j, p, side).wait_send()

            @pl.when(c == 1)
            def _():
                core_share(j, p, side).wait_send()
        return carry

    lax.fori_loop(0, 4 * NC, sent, 0)


def per_device(normed, cotangent, w_in, w_out):
    vmem = pl.BlockSpec(memory_space=pltpu.VMEM)
    hbm = pl.BlockSpec(memory_space=pltpu.HBM)
    two = lambda *shape: [pltpu.SemaphoreType.DMA(shape)] * 2
    inputs = (normed, cotangent, w_in, w_out.reshape(4, NC, Q, DM))
    ng, win_t, wout = pl.pallas_call(
        kernel,
        out_shape=(
            jax.ShapeDtypeStruct((ROWS, DM), BF16),
            jax.ShapeDtypeStruct((FH // 4, DM), F32),
            jax.ShapeDtypeStruct((FH // 4, DM), F32),
        ),
        in_specs=[hbm, hbm, hbm, hbm],
        out_specs=[vmem, vmem, vmem],
        scratch_shapes=[
            pltpu.VMEM((2, 4, 4, ROWS, DM), BF16),
            pltpu.VMEM((DM, FH), BF16),
            pltpu.VMEM((NC, 4, Q, DM), BF16),
            pltpu.VMEM((NC, 4, Q, DM), BF16),
            pltpu.VMEM((NC, 4, 2, 2, 2 * Q, GROUP), BF16),
            pltpu.VMEM((NC, 4, 2, 2, 2 * Q, GROUP), BF16),
            pltpu.VMEM((NC, 4, 2, 2, 2, 2 * Q, GROUP), BF16),
            pltpu.VMEM((2, NC, 4, 2, 2 * Q, GROUP), BF16),
            pltpu.VMEM((NC, 2, 4, Q, DM), BF16),
            pltpu.VMEM((NC, 2, Q, DM), BF16),
            pltpu.VMEM((NC, 2, 2, Q, DM), BF16),
            pltpu.VMEM((4, 4, ROWS, DM), BF16),
            pltpu.VMEM((4, 3, ROWS, DM), BF16),
            pltpu.VMEM((4, ROWS, DM), BF16),
            pltpu.VMEM((3, ROWS, DM), BF16),
            pltpu.SemaphoreType.DMA((7,)),
            *two(2, 2, 2), *two(2, 2), *two(4, 3, 2, 2),
            *two(NC, 4), *two(NC, 4, 2), *two(NC, 4, 2), *two(NC, 4, 2), *two(NC, 4, 2), *two(NC, 4, 2),
            *two(NC, 2), *two(NC, 2),
            *two(4, 3), *two(3),
        ],
        compiler_params=pltpu.CompilerParams(
            collective_id=0, has_side_effects=True, vmem_limit_bytes=48 * 1024 * 1024
        ),
        name="mlp_branch",
    )(*[pltpu.with_memory_space_constraint(t, pltpu.HBM) for t in inputs])
    return ng, win_t.T, wout


def solution(mesh):
    return jax.shard_map(
        per_device,
        mesh=mesh,
        in_specs=(P(("dp", "mx"), "my"), P(("dp", "mx"), "my"), P("my", "mx"), P("mx", "my")),
        out_specs=(P(("dp", "mx"), "my"), P("my", ("mx", "dp")), P(("mx", "dp"), "my")),
        check_vma=False,
    )
```

```python
import jax
import jax.numpy as jnp
from jax import lax
from jax.experimental import pallas as pl
from jax.experimental.pallas import tpu as pltpu
from jax.sharding import PartitionSpec as P

MESH = pl.DeviceIdType.MESH
BF16, F32 = jnp.bfloat16, jnp.float32

NC = 3
ROWS = 32
PIECE = ROWS // 2
GROUP = 4 * ROWS
TOK = 4 * GROUP
DM = 768
FH = 768
FC = FH // NC
Q = FC // 4

K_OF_P = (0, 3, 1, 2)
P_OF_K = (0, 2, 3, 1)
STEP = (1, 3, 2)
FROM = (3, 1, 2)

UNITS = ((0, 0), (0, 1), (0, 2), (1, 0), (2, 0), (1, 1), (3, 0), (3, 1), (2, 1), (3, 2), (1, 2), (2, 2))
GROUP_CODE = sum(p << (2 * n) for n, (p, j) in enumerate(UNITS))
CHUNK_CODE = sum(j << (2 * n) for n, (p, j) in enumerate(UNITS))
GROUP_FIRST = [min(n for n, u in enumerate(UNITS) if u[0] == p) for p in range(4)]
GROUP_LAST = [max(n for n, u in enumerate(UNITS) if u[0] == p) for p in range(4)]
CHUNK_LAST = [max(n for n, u in enumerate(UNITS) if u[1] == j) for j in range(NC)]

SP = 3
S_ADD, S_RELAY, S_FINISH, S_BACK, S_FAR = 1, 1 + SP, 1 + 2 * SP, 1 + 3 * SP, 1 + 4 * SP
S_BWD = S_FAR + 1
STEPS = len(UNITS) + S_BWD
X_STEP2 = 3
Y_SUM = 4


def nt(a, b):
    return lax.dot_general(a, b, (((1,), (1,)), ((), ())), preferred_element_type=F32)


def nn(a, b):
    return lax.dot_general(a, b, (((1,), (0,)), ((), ())), preferred_element_type=F32)


def tn(a, b):
    return lax.dot_general(a, b, (((0,), (0,)), ((), ())), preferred_element_type=F32)


def activate(preact, upstream):
    cumulative = 0.5 * (1.0 + lax.erf(preact * 0.7071067811865476))
    density = jnp.exp(-0.5 * preact * preact) * 0.3989422804014327
    activation = (preact * cumulative).astype(BF16)
    hidden_grad = (upstream * (cumulative + preact * density)).astype(BF16)
    return activation, hidden_grad


def kernel(
    normed, cotangent, w_in, w_out,
    ng_out, grads_out,
    xg, win_v, w1t, wo, pu, crecv, zrecv, ah, dw, xr1, xr2, ngb, yr, zs, zr,
    lsem, az_s, az_r, azf_s, azf_r, ay_s, ay_r, ayf_s, ayf_r,
    co_s, co_r, ne_s, ne_r, ch_s, ch_r, sn_s, sn_r, sp_s, sp_r, ce_s, ce_r, x1_s, x1_r, x2_s, x2_r,
    gy_s, gy_r, gz_s, gz_r,
):
    x = lax.axis_index("dp")
    mx = lax.axis_index("mx")
    my = lax.axis_index("my")
    zh, y = mx // 4, mx % 4
    zl, c = my // 2, my % 2

    def at_x(k):
        return {"dp": (x + k) % 4}

    def at_y(k):
        return {"mx": zh * 4 + (y + k) % 4}

    def at_zh(k):
        return {"mx": ((zh + k) % 4) * 4 + y}

    def at_zl(k):
        return {"my": ((zl + k) % 4) * 2 + c}

    at_core = {"my": zl * 2 + 1 - c}

    def rc(src, dst, send, recv, device):
        return pltpu.make_async_remote_copy(
            src_ref=src, dst_ref=dst, send_sem=send, recv_sem=recv, device_id=device, device_id_type=MESH
        )

    load_own = [pltpu.make_async_copy(t, xg.at[a, 0, 0], lsem.at[5 + a]) for a, t in enumerate((normed, cotangent))]
    load_in = pltpu.make_async_copy(w_in, win_v, lsem.at[4])
    load_out = [pltpu.make_async_copy(w_out.at[g], wo.at[:, g], lsem.at[g]) for g in range(4)]
    for copy in (*load_own, load_in, *load_out):
        copy.start()

    barrier = pltpu.get_barrier_semaphore()
    partners = [at_core, at_y(2), at_zh(2)]
    for k in (1, 3):
        partners += [at_x(k), at_y(k), at_zh(k), at_zl(k)]
    for device in partners:
        pl.semaphore_signal(barrier, inc=1, device_id=device, device_id_type=MESH)
    pl.semaphore_wait(barrier, len(partners))

    def rows(a, p, yy, r):
        return xg.at[a, p, yy, pl.ds(r * PIECE, PIECE)]

    def az(d, a, r):
        there = rows(a, P_OF_K[FROM[d]], 0, r)
        return rc(rows(a, 0, 0, r), there, az_s.at[d, a, r], az_r.at[d, a, r], at_zh(STEP[d]))

    def azf(d, r):
        here = rows(d, P_OF_K[FROM[d]], 0, r)
        return rc(here, rows(d, 3, 0, r), azf_s.at[d, r], azf_r.at[d, r], at_zh(STEP[d]))

    def ay(p, d, a, r):
        there = rows(a, p, FROM[d], r)
        return rc(rows(a, p, 0, r), there, ay_s.at[p, d, a, r], ay_r.at[p, d, a, r], at_y(STEP[d]))

    def ayf(d, r):
        return rc(rows(d, 0, FROM[d], r), rows(d, 0, 2, r), ayf_s.at[d, r], ayf_r.at[d, r], at_y(STEP[d]))

    def along_y(p, a, r):
        for d in (2, 0, 1) if p > 0 else (a, 1 - a):
            ay(p, d, a, r).start()

    def group_here(p):
        for a in range(2):
            for r in range(2):
                ay(p, 1 - a, a, r).wait_recv()
                if p > 0:
                    ay(p, a, a, r).wait_recv()
                    ay(p, 2, a, r).wait_recv()
                else:
                    ayf(a, r).wait_recv()

    for copy in load_own:
        copy.wait()
    for a in range(2):
        for r in range(2):
            az(0, a, r).start()
            az(1, 1 - a, r).start()
    for a in range(2):
        for r in range(2):
            along_y(0, a, r)

    load_in.wait()
    for k in range(FH // 128):
        turned = win_v[:, k * 128:(k + 1) * 128].T
        for u in range(0, 128, 32):
            g, rest = divmod(k * 128 + u, FH // 4)
            w1t[rest // Q, g, pl.ds(rest % Q, 32)] = turned[u:u + 32]
    for copy in load_out:
        copy.wait()

    WAVES = [[(0, 0, r), (1, 1, r)] for r in range(2)] + [[(0, 1, r), (1, 0, r)] for r in range(2)]

    def wave(w):
        if w < 4:
            for d, a, r in WAVES[w]:
                az(d, a, r).wait_recv()
                if d == a:
                    azf(d, r).start()
                along_y(P_OF_K[FROM[d]], a, r)
        else:
            for d in range(2):
                azf(d, w - 4).wait_recv()
                along_y(3, d, w - 4)

    for r in range(2):
        for a in range(2):
            ay(0, a, a, r).wait_recv()
            ayf(a, r).start()
    wave(0)
    wave(1)
    group_here(0)
    wave(2)

    NEAR, OWNER, RELAY, FAR = range(4)

    def place(side):
        return zl if side == 0 else 3 - zl

    def core_copy(j, p):
        return rc(pu.at[j, p], crecv.at[j, p], co_s.at[j, p], co_r.at[j, p], at_core)

    def near(j, p, side):
        there = zrecv.at[j, p, side, 0]
        return rc(pu.at[j, p, side], there, ne_s.at[j, p, side], ne_r.at[j, p, side], at_zl(STEP[side]))

    def chain(j, p, side):
        there = zrecv.at[j, p, side, 1]
        return rc(pu.at[j, p, side], there, ch_s.at[j, p, side], ch_r.at[j, p, side], at_zl(STEP[1 - side]))

    def spread_near(j, p, side):
        here = ah.at[:, j, p, side]
        return rc(here, here, sn_s.at[j, p, side], sn_r.at[j, p, side], at_zl(STEP[1 - side]))

    def spread(j, p, side):
        here = ah.at[:, j, p, side]
        return rc(here, here, sp_s.at[j, p, side], sp_r.at[j, p, side], at_zl(STEP[side]))

    def core_share(j, p, side):
        here = ah.at[:, j, p, side]
        return rc(here, here, ce_s.at[j, p, side], ce_r.at[j, p, side], at_core)

    def x1(j, d):
        return rc(dw.at[j, d, (x + 2) % 4], xr1.at[j, d], x1_s.at[j, d], x1_r.at[j, d], at_x(STEP[d]))

    def x2(j, d):
        return rc(dw.at[j, :, (x + STEP[d]) % 4], xr2.at[j, d], x2_s.at[j, d], x2_r.at[j, d], at_x(STEP[d]))

    def along_gy(p, d):
        return rc(ngb.at[p, STEP[d]], yr.at[p, d], gy_s.at[p, d], gy_r.at[p, d], at_y(STEP[d]))

    def along_gz(d):
        return rc(zs.at[P_OF_K[STEP[d]]], zr.at[d], gz_s.at[d], gz_r.at[d], at_zh(STEP[d]))

    def forward(j, p):
        for a, w in enumerate((w1t, wo)):
            part = nt(w[j].reshape(FC, DM), xg[a, p].reshape(GROUP, DM)).astype(BF16)
            for side in range(2):
                pu[j, p, side, a] = part[side * 2 * Q:(side + 1) * 2 * Q]

        @pl.when(c == 0)
        def _():
            core_copy(j, p).start()

    def add_core(j, p):
        core_copy(j, p).wait_recv()
        pu[j, p] = (pu[j, p].astype(F32) + crecv[j, p].astype(F32)).astype(BF16)
        for side in range(2):
            @pl.when(place(side) == FAR)
            def _():
                chain(j, p, side).start()
                near(j, p, 1 - side).start()

    def pass_on(j, p, side):
        chain(j, p, side).wait_recv()
        pu[j, p, side] = (pu[j, p, side].astype(F32) + zrecv[j, p, side, 1].astype(F32)).astype(BF16)
        chain(j, p, side).start()

    def finish(j, p, side):
        near(j, p, side).wait_recv()
        chain(j, p, side).wait_recv()
        total = pu[j, p, side].astype(F32) + zrecv[j, p, side, 0].astype(F32) + zrecv[j, p, side, 1].astype(F32)
        for a, value in enumerate(activate(total[0], total[1])):
            ah[a, j, p, side] = value
        spread(j, p, side).start()
        spread_near(j, p, side).start()
        core_share(j, p, side).start()

    def pass_back(j, p, side):
        spread(j, p, side).wait_recv()
        spread(j, p, side).start()
        core_share(j, p, side).start()

    def take_far(j, p, side):
        spread(j, p, side).wait_recv()
        core_share(j, p, side).start()

    def take_near(j, p, side):
        spread_near(j, p, side).wait_recv()
        core_share(j, p, side).start()

    def units(a, j):
        return jnp.concatenate([ah[a, j, p].reshape(FC, GROUP) for p in range(4)], axis=1)

    def take_shares(j, p):
        for side in range(2):
            core_share(j, p, side).wait_recv()

    def weight_grads(j, p):
        for d in range(2):
            dw[j, d] = nn(units(1 - d, j), xg[d].reshape(TOK, DM)).astype(BF16).reshape(4, Q, DM)
            x1(j, d).start()

    def normed_grad(j, p):
        total = tn(ah[1, :, p].reshape(FH, GROUP), w1t[...].reshape(FH, DM)).astype(BF16)
        ngb[p] = total.reshape(4, ROWS, DM)
        for d in (2, 0, 1):
            along_gy(p, d).start()

    def x_step2(j):
        for d in range(2):
            x1(j, d).wait_recv()
            to = (x + STEP[d]) % 4
            dw[j, d, to] = (dw[j, d, to].astype(F32) + xr1[j, d].astype(F32)).astype(BF16)
            x2(j, d).start()

    def x_step3(j):
        for d in range(2):
            x2(j, d).wait_recv()
        for a in range(2):
            grads_out[a, j * Q:(j + 1) * Q] = (
                dw[j, a, x].astype(F32) + xr2[j, 0, a].astype(F32) + xr2[j, 1, a].astype(F32)
            )

    def sum_y(p):
        total = ngb[p, 0].astype(F32)
        for d in range(3):
            along_gy(p, d).wait_recv()
            total = total + yr[p, d].astype(F32)
        zs[p] = total.astype(BF16)
        for d in range(3):
            if P_OF_K[STEP[d]] == p:
                along_gz(d).start()

    AHEAD = {0: lambda: wave(3), 1: lambda: wave(4), 2: lambda: wave(5)}

    def step(tau, carry):
        def stage(s, run, on=None, core=None, among=None):
            slot = tau - s
            here = (slot >= 0) & (slot < len(UNITS))
            if on is not None:
                here = here & (c == 1) & (place(on[0]) == on[1])
            if core is not None:
                here = here & (c == core)
            if among is not None:
                here = sum(jnp.where(slot == n, 1, 0) for n in among) > 0

            @pl.when(here)
            def _():
                j, p = ((code >> (2 * slot)) & 3 for code in (CHUNK_CODE, GROUP_CODE))
                run(j, p)

        def at(n, run):
            @pl.when(tau == n)
            def _():
                run()

        for n, run in AHEAD.items():
            at(n, run)
        for side in range(2):
            stage(S_FAR, lambda j, p: take_far(j, p, side), (side, FAR))
            stage(S_BACK, lambda j, p: pass_back(j, p, side), (side, RELAY))
            stage(S_BACK, lambda j, p: take_near(j, p, side), (side, NEAR))
        for side in range(2):
            stage(S_FINISH, lambda j, p: finish(j, p, side), (side, OWNER))
        for side in range(2):
            stage(S_RELAY, lambda j, p: pass_on(j, p, side), (side, RELAY))
        stage(S_ADD, add_core, core=1)
        for p in range(1, 4):
            at(GROUP_FIRST[p], lambda: group_here(p))
        stage(0, forward)
        stage(S_BWD, take_shares, core=0)
        stage(S_BWD, weight_grads, among=CHUNK_LAST)
        stage(S_BWD, normed_grad, among=GROUP_LAST)
        for j in range(NC):
            at(CHUNK_LAST[j] + S_BWD + X_STEP2, lambda: x_step2(j))
        for p in range(4):
            at(GROUP_LAST[p] + S_BWD + Y_SUM, lambda: sum_y(p))
        return carry

    lax.fori_loop(0, STEPS, step, 0)

    def rest_x(j):
        if CHUNK_LAST[j] + S_BWD + X_STEP2 >= STEPS:
            x_step2(j)

    def rest_y(p):
        if GROUP_LAST[p] + S_BWD + Y_SUM >= STEPS:
            sum_y(p)

    rest_y(0)
    rest_y(3)
    rest_x(0)
    rest_x(1)
    rest_y(1)
    rest_x(2)
    rest_y(2)
    x_step3(0)
    x_step3(1)
    total = zs[0].astype(F32)
    for d in (2, 0, 1):
        along_gz(d).wait_recv()
        total = total + zr[d].astype(F32)
    ng_out[...] = total.astype(BF16)
    x_step3(2)

    for d in range(3):
        for p in range(4):
            for a in range(2):
                for r in range(2):
                    if d < 2 or p > 0:
                        ay(p, d, a, r).wait_send()
            along_gy(p, d).wait_send()
        along_gz(d).wait_send()
    for d in range(2):
        for r in range(2):
            for a in range(2):
                az(d, a, r).wait_send()
            azf(d, r).wait_send()
            ayf(d, r).wait_send()
        for j in range(NC):
            x1(j, d).wait_send()
            x2(j, d).wait_send()

    def sent(u, carry):
        j, p = u % NC, u // NC
        @pl.when(c == 0)
        def _():
            core_copy(j, p).wait_send()

        for side in range(2):
            here = place(side)

            @pl.when((c == 1) & (here == NEAR))
            def _():
                near(j, p, side).wait_send()

            @pl.when((c == 1) & (here >= RELAY))
            def _():
                chain(j, p, side).wait_send()

            @pl.when((c == 1) & (here == OWNER))
            def _():
                spread_near(j, p, side).wait_send()

            @pl.when((c == 1) & ((here == OWNER) | (here == RELAY)))
            def _():
                spread(j, p, side).wait_send()

            @pl.when(c == 1)
            def _():
                core_share(j, p, side).wait_send()
        return carry

    lax.fori_loop(0, 4 * NC, sent, 0)


def per_device(normed, cotangent, w_in, w_out):
    vmem = pl.BlockSpec(memory_space=pltpu.VMEM)
    hbm = pl.BlockSpec(memory_space=pltpu.HBM)
    two = lambda *shape: [pltpu.SemaphoreType.DMA(shape)] * 2
    inputs = (normed, cotangent, w_in, w_out.reshape(4, NC, Q, DM))
    ng, grads = pl.pallas_call(
        kernel,
        out_shape=(
            jax.ShapeDtypeStruct((ROWS, DM), BF16),
            jax.ShapeDtypeStruct((2, FH // 4, DM), F32),
        ),
        in_specs=[hbm, hbm, hbm, hbm],
        out_specs=[vmem, vmem],
        scratch_shapes=[
            pltpu.VMEM((2, 4, 4, ROWS, DM), BF16),
            pltpu.VMEM((DM, FH), BF16),
            pltpu.VMEM((NC, 4, Q, DM), BF16),
            pltpu.VMEM((NC, 4, Q, DM), BF16),
            pltpu.VMEM((NC, 4, 2, 2, 2 * Q, GROUP), BF16),
            pltpu.VMEM((NC, 4, 2, 2, 2 * Q, GROUP), BF16),
            pltpu.VMEM((NC, 4, 2, 2, 2, 2 * Q, GROUP), BF16),
            pltpu.VMEM((2, NC, 4, 2, 2 * Q, GROUP), BF16),
            pltpu.VMEM((NC, 2, 4, Q, DM), BF16),
            pltpu.VMEM((NC, 2, Q, DM), BF16),
            pltpu.VMEM((NC, 2, 2, Q, DM), BF16),
            pltpu.VMEM((4, 4, ROWS, DM), BF16),
            pltpu.VMEM((4, 3, ROWS, DM), BF16),
            pltpu.VMEM((4, ROWS, DM), BF16),
            pltpu.VMEM((3, ROWS, DM), BF16),
            pltpu.SemaphoreType.DMA((7,)),
            *two(2, 2, 2), *two(2, 2), *two(4, 3, 2, 2), *two(2, 2),
            *two(NC, 4), *two(NC, 4, 2), *two(NC, 4, 2), *two(NC, 4, 2), *two(NC, 4, 2), *two(NC, 4, 2),
            *two(NC, 2), *two(NC, 2),
            *two(4, 3), *two(3),
        ],
        compiler_params=pltpu.CompilerParams(
            collective_id=0, has_side_effects=True, vmem_limit_bytes=48 * 1024 * 1024
        ),
        name="mlp_branch",
    )(*[pltpu.with_memory_space_constraint(t, pltpu.HBM) for t in inputs])
    return ng, grads[0].T, grads[1]


def solution(mesh):
    return jax.shard_map(
        per_device,
        mesh=mesh,
        in_specs=(P(("dp", "mx"), "my"), P(("dp", "mx"), "my"), P("my", "mx"), P("mx", "my")),
        out_specs=(P(("dp", "mx"), "my"), P("my", ("mx", "dp")), P(("mx", "dp"), "my")),
        check_vma=False,
    )
```

```python
import jax
import jax.numpy as jnp
from jax import lax
from jax.experimental import pallas as pl
from jax.experimental.pallas import tpu as pltpu
from jax.sharding import PartitionSpec as P

MESH = pl.DeviceIdType.MESH
BF16, F32 = jnp.bfloat16, jnp.float32

NC = 3
ROWS = 32
PIECE = ROWS // 2
GROUP = 4 * ROWS
TOK = 4 * GROUP
DM = 768
FH = 768
FC = FH // NC
Q = FC // 4

K_OF_P = (0, 3, 1, 2)
P_OF_K = (0, 2, 3, 1)
STEP = (1, 3, 2)
FROM = (3, 1, 2)

UNITS = ((0, 0), (0, 1), (0, 2), (1, 0), (2, 0), (1, 1), (3, 0), (3, 1), (2, 1), (3, 2), (1, 2), (2, 2))
GROUP_CODE = sum(p << (2 * n) for n, (p, j) in enumerate(UNITS))
CHUNK_CODE = sum(j << (2 * n) for n, (p, j) in enumerate(UNITS))
GROUP_FIRST = [min(n for n, u in enumerate(UNITS) if u[0] == p) for p in range(4)]
GROUP_LAST = [max(n for n, u in enumerate(UNITS) if u[0] == p) for p in range(4)]
CHUNK_LAST = [max(n for n, u in enumerate(UNITS) if u[1] == j) for j in range(NC)]

SP = 3
S_ADD, S_RELAY, S_FINISH, S_BACK, S_FAR = 1, 1 + SP, 1 + 2 * SP, 1 + 3 * SP, 1 + 4 * SP
S_BWD = S_FAR + 1
STEPS = len(UNITS) + S_BWD
X_STEP2 = 3
Y_SUM = 4


def nt(a, b):
    return lax.dot_general(a, b, (((1,), (1,)), ((), ())), preferred_element_type=F32)


def nn(a, b):
    return lax.dot_general(a, b, (((1,), (0,)), ((), ())), preferred_element_type=F32)


def tn(a, b):
    return lax.dot_general(a, b, (((0,), (0,)), ((), ())), preferred_element_type=F32)


def activate(preact, upstream):
    cumulative = 0.5 * (1.0 + lax.erf(preact * 0.7071067811865476))
    density = jnp.exp(-0.5 * preact * preact) * 0.3989422804014327
    activation = (preact * cumulative).astype(BF16)
    hidden_grad = (upstream * (cumulative + preact * density)).astype(BF16)
    return activation, hidden_grad


def kernel(
    normed, cotangent, w_in, w_out,
    ng_out, grads_out,
    xg, win_v, w1t, wo, pu, crecv, zrecv, ah, dw, xr1, xr2, ngb, yr, zs, zr,
    lsem, az_s, az_r, azf_s, azf_r, ay_s, ay_r, ayf_s, ayf_r,
    co_s, co_r, ne_s, ne_r, ch_s, ch_r, sn_s, sn_r, sp_s, sp_r, ce_s, ce_r, x1_s, x1_r, x2_s, x2_r,
    gy_s, gy_r, gz_s, gz_r,
):
    x = lax.axis_index("dp")
    mx = lax.axis_index("mx")
    my = lax.axis_index("my")
    zh, y = mx // 4, mx % 4
    zl, c = my // 2, my % 2

    def at_x(k):
        return {"dp": (x + k) % 4}

    def at_y(k):
        return {"mx": zh * 4 + (y + k) % 4}

    def at_zh(k):
        return {"mx": ((zh + k) % 4) * 4 + y}

    def at_zl(k):
        return {"my": ((zl + k) % 4) * 2 + c}

    at_core = {"my": zl * 2 + 1 - c}

    def rc(src, dst, send, recv, device):
        return pltpu.make_async_remote_copy(
            src_ref=src, dst_ref=dst, send_sem=send, recv_sem=recv, device_id=device, device_id_type=MESH
        )

    load_own = [pltpu.make_async_copy(t, xg.at[a, 0, 0], lsem.at[5 + a]) for a, t in enumerate((normed, cotangent))]
    load_in = pltpu.make_async_copy(w_in, win_v, lsem.at[4])
    load_out = [pltpu.make_async_copy(w_out.at[g], wo.at[:, g], lsem.at[g]) for g in range(4)]
    for copy in (*load_own, load_in, *load_out):
        copy.start()

    barrier = pltpu.get_barrier_semaphore()
    partners = [at_core, at_y(2), at_zh(2)]
    for k in (1, 3):
        partners += [at_x(k), at_y(k), at_zh(k), at_zl(k)]
    for device in partners:
        pl.semaphore_signal(barrier, inc=1, device_id=device, device_id_type=MESH)
    pl.semaphore_wait(barrier, len(partners))

    def rows(a, p, yy, r):
        return xg.at[a, p, yy, pl.ds(r * PIECE, PIECE)]

    def az(d, a, r):
        there = rows(a, P_OF_K[FROM[d]], 0, r)
        return rc(rows(a, 0, 0, r), there, az_s.at[d, a, r], az_r.at[d, a, r], at_zh(STEP[d]))

    def azf(d, r):
        here = rows(d, P_OF_K[FROM[d]], 0, r)
        return rc(here, rows(d, 3, 0, r), azf_s.at[d, r], azf_r.at[d, r], at_zh(STEP[d]))

    def ay(p, d, a, r):
        there = rows(a, p, FROM[d], r)
        return rc(rows(a, p, 0, r), there, ay_s.at[p, d, a, r], ay_r.at[p, d, a, r], at_y(STEP[d]))

    def ayf(d, r):
        return rc(rows(d, 0, FROM[d], r), rows(d, 0, 2, r), ayf_s.at[d, r], ayf_r.at[d, r], at_y(STEP[d]))

    def along_y(p, a, r):
        for d in (2, 0, 1) if p > 0 else (a, 1 - a):
            ay(p, d, a, r).start()

    def group_here(p):
        for a in range(2):
            for r in range(2):
                ay(p, 1 - a, a, r).wait_recv()
                if p > 0:
                    ay(p, a, a, r).wait_recv()
                    ay(p, 2, a, r).wait_recv()
                else:
                    ayf(a, r).wait_recv()

    for copy in load_own:
        copy.wait()
    for a in range(2):
        for r in range(2):
            az(0, a, r).start()
            az(1, 1 - a, r).start()
    for a in range(2):
        for r in range(2):
            along_y(0, a, r)

    load_in.wait()
    for k in range(FH // 128):
        turned = win_v[:, k * 128:(k + 1) * 128].T
        for u in range(0, 128, 32):
            g, rest = divmod(k * 128 + u, FH // 4)
            w1t[rest // Q, g, pl.ds(rest % Q, 32)] = turned[u:u + 32]
    for copy in load_out:
        copy.wait()

    WAVES = [[(0, 0, r), (1, 1, r)] for r in range(2)] + [[(0, 1, r), (1, 0, r)] for r in range(2)]

    def wave(w):
        if w < 4:
            for d, a, r in WAVES[w]:
                az(d, a, r).wait_recv()
                if d == a:
                    azf(d, r).start()
                along_y(P_OF_K[FROM[d]], a, r)
        else:
            for d in range(2):
                azf(d, w - 4).wait_recv()
                along_y(3, d, w - 4)

    for r in range(2):
        for a in range(2):
            ay(0, a, a, r).wait_recv()
            ayf(a, r).start()
    wave(0)
    wave(1)
    group_here(0)
    wave(2)

    NEAR, OWNER, RELAY, FAR = range(4)

    def place(side):
        return zl if side == 0 else 3 - zl

    def core_copy(j, p):
        return rc(pu.at[j, p], crecv.at[j, p], co_s.at[j, p], co_r.at[j, p], at_core)

    def near(j, p, side):
        there = zrecv.at[j, p, side, 0]
        return rc(pu.at[j, p, side], there, ne_s.at[j, p, side], ne_r.at[j, p, side], at_zl(STEP[side]))

    def chain(j, p, side):
        there = zrecv.at[j, p, side, 1]
        return rc(pu.at[j, p, side], there, ch_s.at[j, p, side], ch_r.at[j, p, side], at_zl(STEP[1 - side]))

    def spread_near(j, p, side):
        here = ah.at[:, j, p, side]
        return rc(here, here, sn_s.at[j, p, side], sn_r.at[j, p, side], at_zl(STEP[1 - side]))

    def spread(j, p, side):
        here = ah.at[:, j, p, side]
        return rc(here, here, sp_s.at[j, p, side], sp_r.at[j, p, side], at_zl(STEP[side]))

    def core_share(j, p, side):
        here = ah.at[:, j, p, side]
        return rc(here, here, ce_s.at[j, p, side], ce_r.at[j, p, side], at_core)

    def x1(j, d):
        return rc(dw.at[j, d, (x + 2) % 4], xr1.at[j, d], x1_s.at[j, d], x1_r.at[j, d], at_x(STEP[d]))

    def x2(j, d):
        return rc(dw.at[j, :, (x + STEP[d]) % 4], xr2.at[j, d], x2_s.at[j, d], x2_r.at[j, d], at_x(STEP[d]))

    def along_gy(p, d):
        return rc(ngb.at[p, STEP[d]], yr.at[p, d], gy_s.at[p, d], gy_r.at[p, d], at_y(STEP[d]))

    def along_gz(d):
        return rc(zs.at[P_OF_K[STEP[d]]], zr.at[d], gz_s.at[d], gz_r.at[d], at_zh(STEP[d]))

    def forward(j, p):
        for a, w in enumerate((w1t, wo)):
            part = nt(w[j].reshape(FC, DM), xg[a, p].reshape(GROUP, DM)).astype(BF16)
            for side in range(2):
                pu[j, p, side, a] = part[side * 2 * Q:(side + 1) * 2 * Q]

        @pl.when(c == 0)
        def _():
            core_copy(j, p).start()

    def add_core(j, p):
        core_copy(j, p).wait_recv()
        pu[j, p] = (pu[j, p].astype(F32) + crecv[j, p].astype(F32)).astype(BF16)
        for side in range(2):
            @pl.when(place(side) == FAR)
            def _():
                chain(j, p, side).start()
                near(j, p, 1 - side).start()

    def pass_on(j, p, side):
        chain(j, p, side).wait_recv()
        pu[j, p, side] = (pu[j, p, side].astype(F32) + zrecv[j, p, side, 1].astype(F32)).astype(BF16)
        chain(j, p, side).start()

    def finish(j, p, side):
        near(j, p, side).wait_recv()
        chain(j, p, side).wait_recv()
        total = pu[j, p, side].astype(F32) + zrecv[j, p, side, 0].astype(F32) + zrecv[j, p, side, 1].astype(F32)
        for a, value in enumerate(activate(total[0], total[1])):
            ah[a, j, p, side] = value
        spread(j, p, side).start()
        spread_near(j, p, side).start()
        core_share(j, p, side).start()

    def pass_back(j, p, side):
        spread(j, p, side).wait_recv()
        spread(j, p, side).start()
        core_share(j, p, side).start()

    def take_far(j, p, side):
        spread(j, p, side).wait_recv()
        core_share(j, p, side).start()

    def take_near(j, p, side):
        spread_near(j, p, side).wait_recv()
        core_share(j, p, side).start()

    def units(a, j):
        return jnp.concatenate([ah[a, j, p].reshape(FC, GROUP) for p in range(4)], axis=1)

    def take_shares(j, p):
        for side in range(2):
            core_share(j, p, side).wait_recv()

    def weight_grads(j, p):
        for d in range(2):
            dw[j, d] = nn(units(1 - d, j), xg[d].reshape(TOK, DM)).astype(BF16).reshape(4, Q, DM)
            x1(j, d).start()

    def normed_grad(j, p):
        total = tn(ah[1, :, p].reshape(FH, GROUP), w1t[...].reshape(FH, DM)).astype(BF16)
        ngb[p] = total.reshape(4, ROWS, DM)
        for d in (2, 0, 1):
            along_gy(p, d).start()

    def x_step2(j):
        for d in range(2):
            x1(j, d).wait_recv()
            to = (x + STEP[d]) % 4
            dw[j, d, to] = (dw[j, d, to].astype(F32) + xr1[j, d].astype(F32)).astype(BF16)
            x2(j, d).start()

    def x_step3(j):
        for d in range(2):
            x2(j, d).wait_recv()
        for a in range(2):
            grads_out[a, j * Q:(j + 1) * Q] = (
                dw[j, a, x].astype(F32) + xr2[j, 0, a].astype(F32) + xr2[j, 1, a].astype(F32)
            )

    def sum_y(p):
        total = ngb[p, 0].astype(F32)
        for d in range(3):
            along_gy(p, d).wait_recv()
            total = total + yr[p, d].astype(F32)
        zs[p] = total.astype(BF16)
        for d in range(3):
            if P_OF_K[STEP[d]] == p:
                along_gz(d).start()

    AHEAD = {0: lambda: wave(3), 1: lambda: wave(4), 2: lambda: wave(5)}

    def step(tau, carry):
        def stage(s, run, on=None, core=None, among=None):
            slot = tau - s
            here = (slot >= 0) & (slot < len(UNITS))
            if on is not None:
                here = here & (c == 1) & (place(on[0]) == on[1])
            if core is not None:
                here = here & (c == core)
            if among is not None:
                here = sum(jnp.where(slot == n, 1, 0) for n in among) > 0

            @pl.when(here)
            def _():
                j, p = ((code >> (2 * slot)) & 3 for code in (CHUNK_CODE, GROUP_CODE))
                run(j, p)

        def at(n, run):
            @pl.when(tau == n)
            def _():
                run()

        for n, run in AHEAD.items():
            at(n, run)
        for side in range(2):
            stage(S_FAR, lambda j, p: take_far(j, p, side), (side, FAR))
            stage(S_BACK, lambda j, p: pass_back(j, p, side), (side, RELAY))
            stage(S_BACK, lambda j, p: take_near(j, p, side), (side, NEAR))
        for side in range(2):
            stage(S_FINISH, lambda j, p: finish(j, p, side), (side, OWNER))
        for side in range(2):
            stage(S_RELAY, lambda j, p: pass_on(j, p, side), (side, RELAY))
        stage(S_ADD, add_core, core=1)
        for p in range(1, 4):
            at(GROUP_FIRST[p], lambda: group_here(p))
        stage(0, forward)
        stage(S_BWD, take_shares, core=0)
        stage(S_BWD, weight_grads, among=CHUNK_LAST)
        stage(S_BWD, normed_grad, among=GROUP_LAST)
        for j in range(NC):
            at(CHUNK_LAST[j] + S_BWD + X_STEP2, lambda: x_step2(j))
        for p in range(4):
            at(GROUP_LAST[p] + S_BWD + Y_SUM, lambda: sum_y(p))
        return carry

    lax.fori_loop(0, STEPS, step, 0)

    def rest_x(j):
        if CHUNK_LAST[j] + S_BWD + X_STEP2 >= STEPS:
            x_step2(j)

    def rest_y(p):
        if GROUP_LAST[p] + S_BWD + Y_SUM >= STEPS:
            sum_y(p)

    rest_y(0)
    rest_y(3)
    rest_x(0)
    rest_x(1)
    rest_y(1)
    rest_x(2)
    rest_y(2)
    for d in range(3):
        for p in range(4):
            for a in range(2):
                for r in range(2):
                    if d < 2 or p > 0:
                        ay(p, d, a, r).wait_send()
    for d in range(2):
        for r in range(2):
            for a in range(2):
                az(d, a, r).wait_send()
            azf(d, r).wait_send()
            ayf(d, r).wait_send()

    def sent(u, carry):
        j, p = u % NC, u // NC
        @pl.when(c == 0)
        def _():
            core_copy(j, p).wait_send()

        for side in range(2):
            here = place(side)

            @pl.when((c == 1) & (here == NEAR))
            def _():
                near(j, p, side).wait_send()

            @pl.when((c == 1) & (here >= RELAY))
            def _():
                chain(j, p, side).wait_send()

            @pl.when((c == 1) & (here == OWNER))
            def _():
                spread_near(j, p, side).wait_send()

            @pl.when((c == 1) & ((here == OWNER) | (here == RELAY)))
            def _():
                spread(j, p, side).wait_send()

            @pl.when(c == 1)
            def _():
                core_share(j, p, side).wait_send()
        return carry

    lax.fori_loop(0, 4 * NC, sent, 0)

    x_step3(0)
    x_step3(1)
    total = zs[0].astype(F32)
    for d in (2, 0, 1):
        along_gz(d).wait_recv()
        total = total + zr[d].astype(F32)
    ng_out[...] = total.astype(BF16)
    x_step3(2)

    for d in range(3):
        for p in range(4):
            along_gy(p, d).wait_send()
        along_gz(d).wait_send()
    for d in range(2):
        for j in range(NC):
            x1(j, d).wait_send()
            x2(j, d).wait_send()


def per_device(normed, cotangent, w_in, w_out):
    vmem = pl.BlockSpec(memory_space=pltpu.VMEM)
    hbm = pl.BlockSpec(memory_space=pltpu.HBM)
    two = lambda *shape: [pltpu.SemaphoreType.DMA(shape)] * 2
    inputs = (normed, cotangent, w_in, w_out.reshape(4, NC, Q, DM))
    ng, grads = pl.pallas_call(
        kernel,
        out_shape=(
            jax.ShapeDtypeStruct((ROWS, DM), BF16),
            jax.ShapeDtypeStruct((2, FH // 4, DM), F32),
        ),
        in_specs=[hbm, hbm, hbm, hbm],
        out_specs=[vmem, vmem],
        scratch_shapes=[
            pltpu.VMEM((2, 4, 4, ROWS, DM), BF16),
            pltpu.VMEM((DM, FH), BF16),
            pltpu.VMEM((NC, 4, Q, DM), BF16),
            pltpu.VMEM((NC, 4, Q, DM), BF16),
            pltpu.VMEM((NC, 4, 2, 2, 2 * Q, GROUP), BF16),
            pltpu.VMEM((NC, 4, 2, 2, 2 * Q, GROUP), BF16),
            pltpu.VMEM((NC, 4, 2, 2, 2, 2 * Q, GROUP), BF16),
            pltpu.VMEM((2, NC, 4, 2, 2 * Q, GROUP), BF16),
            pltpu.VMEM((NC, 2, 4, Q, DM), BF16),
            pltpu.VMEM((NC, 2, Q, DM), BF16),
            pltpu.VMEM((NC, 2, 2, Q, DM), BF16),
            pltpu.VMEM((4, 4, ROWS, DM), BF16),
            pltpu.VMEM((4, 3, ROWS, DM), BF16),
            pltpu.VMEM((4, ROWS, DM), BF16),
            pltpu.VMEM((3, ROWS, DM), BF16),
            pltpu.SemaphoreType.DMA((7,)),
            *two(2, 2, 2), *two(2, 2), *two(4, 3, 2, 2), *two(2, 2),
            *two(NC, 4), *two(NC, 4, 2), *two(NC, 4, 2), *two(NC, 4, 2), *two(NC, 4, 2), *two(NC, 4, 2),
            *two(NC, 2), *two(NC, 2),
            *two(4, 3), *two(3),
        ],
        compiler_params=pltpu.CompilerParams(
            collective_id=0, has_side_effects=True, vmem_limit_bytes=48 * 1024 * 1024
        ),
        name="mlp_branch",
    )(*[pltpu.with_memory_space_constraint(t, pltpu.HBM) for t in inputs])
    return ng, grads[0].T, grads[1]


def solution(mesh):
    return jax.shard_map(
        per_device,
        mesh=mesh,
        in_specs=(P(("dp", "mx"), "my"), P(("dp", "mx"), "my"), P("my", "mx"), P("mx", "my")),
        out_specs=(P(("dp", "mx"), "my"), P("my", ("mx", "dp")), P(("mx", "dp"), "my")),
        check_vma=False,
    )
```
